256 devices in a mesh: blk: 64 (over y, z, x_hi), rep: 4 (over x_lo, core).
Axes of the slice: x: 4 (x_hi: 2, x_lo: 2; x = x_hi * 2 + x_lo), y: 4, z: 8, core: 2. Of those that a mesh axis runs over, the one named last changes fastest.
Arguments:
- embeddings: bfloat16 [131072, 256], P('blk'), may hold values from -6 to 6
- counts: int32 [64], P('blk'), may hold values from 128 to 2048, as said below
- validity: int32 [131072], P('blk'), may hold values 0 or 1
Outputs:
- log_density: float32 [131072], P('blk')
- mean_embedding: float32 [131072, 256], P('blk', 'rep')
The draws below stay inside these ranges and needn't reach their ends.
Inputs may be any that keep to these rules, and one draw needn't show every extreme that they name: `counts`: every count is a multiple of 128, and some block is full.
All inputs are finite; a program needn't handle non-finite values. No bound on the sum of `validity` on one device may be relied on, other than what follows from the above.
Results may differ from the reference program's by a relative error of at most 0.0047.
Values may be sent and summed in bfloat16 or wider, within the bound.
No kernel may reach another device: no remote copies, remote signals or barrier semaphores. Data moves between devices by JAX's collectives and lax.ppermute only.
A program may use at most 64 MiB of HBM per device.

```python
import jax
import jax.numpy as jnp
from jax import lax

E = 256
ROWS_DEV = 2048
TILE = 128
HOPS = 3
BLOCKS = 64
ROWS = 131072


def draw_counts(key, part):
    key = jax.random.fold_in(key, 1)
    first_key, second_key = jax.random.split(key)
    granules = jax.random.randint(first_key, (BLOCKS,), 1, ROWS_DEV // TILE + 1) * TILE
    chosen = jax.random.randint(second_key, (), 0, BLOCKS)
    return jnp.where(jnp.arange(BLOCKS) == chosen, ROWS_DEV, granules).astype(jnp.int32)


def draw_embeddings(key, part):
    key = jax.random.fold_in(key, 2)
    base_key, target_key, source_key, offset_key, factor_key = jax.random.split(key, 5)
    base = jnp.clip(jax.random.normal(base_key, (BLOCKS, ROWS_DEV, E), jnp.float32), -4.6, 4.6)
    half = TILE // 2
    copies = TILE // 16
    block_index = jnp.arange(BLOCKS, dtype=jnp.int32)
    copy_index = jnp.arange(copies, dtype=jnp.int32)
    target_order = jax.vmap(lambda one: jax.random.permutation(one, half))(jax.random.split(target_key, BLOCKS))
    source_order = jax.vmap(lambda one: jax.random.permutation(one, half))(jax.random.split(source_key, BLOCKS))
    offsets = jax.random.randint(offset_key, (BLOCKS,), 0, HOPS)
    distance = 1 + (copy_index[None, :] + offsets[:, None]) % HOPS
    source_block = (block_index[:, None] - distance) % BLOCKS
    source_slot = half + source_order[source_block, (distance - 1) * copies + copy_index[None, :]]
    target_slot = target_order[:, :copies]
    factor = jnp.exp(jax.random.uniform(factor_key, (BLOCKS, copies), jnp.float32, 0.0, 0.25))
    scaled = base[source_block, source_slot] * factor[:, :, None]
    base = base.at[source_block, source_slot].set(scaled)
    base = base.at[jnp.broadcast_to(block_index[:, None], (BLOCKS, copies)), target_slot].set(scaled)
    return base.reshape(BLOCKS * ROWS_DEV, E).astype(jnp.bfloat16)


def touch_ends(result, rng, least, largest):
    longest = result.shape.index(max(result.shape))
    spots = []
    for shift in (0, 1):
        where = [jax.random.randint(jax.random.fold_in(rng, axis), (), 0, length) for axis, length in enumerate(result.shape)]
        where[longest] = (where[longest] + shift) % result.shape[longest]
        spots.append(tuple(where))
    return result.at[spots[0]].set(least).at[spots[1]].set(largest)


def setup_inputs(seed: int = 0) -> dict:
    key_of = jax.random.split(jax.random.key(seed), 4)
    embeddings = draw_embeddings(jax.random.fold_in(key_of[3], 71), 0)
    counts = draw_counts(jax.random.fold_in(key_of[3], 71), 0)
    validity = touch_ends((jax.random.randint(key_of[2], (ROWS,), 0, 4) < 3).astype(jnp.int32), jax.random.fold_in(key_of[2], 1), 0, 1)
    return {"embeddings": embeddings, "counts": counts, "validity": validity}


BETA = 8.0
EPSILON = 1e-6


def kernel_tile(left, left_live, right, right_live):
    gram = jnp.dot(left, right.T, preferred_element_type=jnp.float32)
    left_square = jnp.sum(jnp.square(left.astype(jnp.float32)), axis=1)
    right_square = jnp.sum(jnp.square(right.astype(jnp.float32)), axis=1)
    distance = left_square[:, None] + right_square[None, :] - 2.0 * gram
    return jnp.exp(BETA * (2.0 - distance / E)) * left_live[:, None] * right_live[None, :]


def reference(embeddings, counts, validity):
    blocks_x = embeddings.reshape(BLOCKS, ROWS_DEV, E)
    position = jnp.arange(ROWS_DEV, dtype=jnp.int32)
    live = ((position[None, :] < counts[:, None]) & (validity.reshape(BLOCKS, ROWS_DEV) == 1)).astype(jnp.float32)
    off_diagonal = 1.0 - jnp.eye(ROWS_DEV, dtype=jnp.float32)

    def one_block(index):
        own = lax.dynamic_index_in_dim(blocks_x, index, 0, keepdims=False)
        own_live = lax.dynamic_index_in_dim(live, index, 0, keepdims=False)
        totals = jnp.zeros((ROWS_DEV,), jnp.float32)
        weighted = jnp.zeros((ROWS_DEV, E), jnp.float32)
        for offset in range(-HOPS, HOPS + 1):
            other_index = ((index + offset) % BLOCKS).astype(jnp.int32)
            other = lax.dynamic_index_in_dim(blocks_x, other_index, 0, keepdims=False)
            other_live = lax.dynamic_index_in_dim(live, other_index, 0, keepdims=False)
            kernel = kernel_tile(own, own_live, other, other_live)
            if offset == 0:
                kernel = kernel * off_diagonal
            totals = totals + jnp.sum(kernel, axis=1)
            weighted = weighted + jnp.dot(kernel.astype(jnp.bfloat16), other, preferred_element_type=jnp.float32)
        return totals, weighted

    totals, weighted = lax.map(one_block, jnp.arange(BLOCKS, dtype=jnp.int32))
    totals = totals.reshape(ROWS)
    log_density = live.reshape(ROWS) * jnp.log(totals + EPSILON)
    mean_embedding = weighted.reshape(ROWS, E) / (totals + EPSILON)[:, None]
    return log_density, mean_embedding
```

```python
import functools
import math

import jax
import jax.numpy as jnp
from jax import lax
from jax.experimental import pallas as pl
from jax.experimental.pallas import tpu as pltpu
from jax.sharding import PartitionSpec as P

BETA = 8.0
EPSILON = 1e-06
LOG2E = math.log2(math.e)
DEAD = -1e30

SLOTS = 2048
WIDTH = 256
SHARE = 512
GRANULE = 128
EXTRA = 16
TILE = 512
PART = 64

F32 = jnp.float32
BF16 = jnp.bfloat16
NT = (((1,), (1,)), ((), ()))
VMEM_LIMIT = 40 * 2**20

CROSS = 2.0 * BETA / WIDTH * LOG2E
ROW = -BETA / WIDTH * LOG2E
TOP = 2.0 * BETA * LOG2E


def split3(value):
    high = value.astype(BF16)
    rest = value - high.astype(F32)
    middle = rest.astype(BF16)
    low = (rest - middle.astype(F32)).astype(BF16)
    return high, middle, low


def pack_body(counts_ref, embeddings_ref, validity_ref, message_ref, sems):
    rep = lax.axis_index("rep")
    copies = []
    for k in range(4):
        start = pl.multiple_of((4 * k + rep) * GRANULE, GRANULE)
        copies.append(
            pltpu.make_async_copy(
                embeddings_ref.at[pl.ds(start, GRANULE), :],
                message_ref.at[pl.ds(k * GRANULE, GRANULE), :],
                sems.at[k],
            )
        )
        copies[-1].start()
    ones = jnp.ones((8, WIDTH), BF16)
    biases = []
    for k in range(4):
        copies[k].wait()
        rows = message_ref[k * GRANULE : (k + 1) * GRANULE, :].astype(F32)
        square = rows * rows
        high = square.astype(BF16)
        low = (square - high.astype(F32)).astype(BF16)
        norm = lax.dot_general(ones, high, NT, preferred_element_type=F32)
        norm = norm + lax.dot_general(ones, low, NT, preferred_element_type=F32)
        granule = 4 * k + rep
        position = granule * GRANULE + lax.broadcasted_iota(jnp.int32, (1, GRANULE), 1)
        valid = validity_ref[pl.ds(granule, 1), :]
        live = (position < counts_ref[0]) & (valid == 1)
        biases.append(jnp.where(live, TOP + ROW * norm[:1], DEAD))
    pairs = [jnp.concatenate(biases[:2], 1), jnp.concatenate(biases[2:], 1)]
    parts = [split3(pair) for pair in pairs]
    lines = [parts[h][level].astype(F32) for level in range(3) for h in range(2)]
    lines.append(jnp.zeros((EXTRA - 6, WIDTH), F32))
    message_ref[SHARE:, :] = jnp.concatenate(lines, 0).astype(BF16)


def pack(embeddings, counts, validity):
    return pl.pallas_call(
        pack_body,
        in_specs=[
            pl.BlockSpec(memory_space=pltpu.SMEM),
            pl.BlockSpec(memory_space=pl.ANY),
            pl.BlockSpec(memory_space=pltpu.VMEM),
        ],
        out_specs=pl.BlockSpec(memory_space=pltpu.VMEM),
        out_shape=jax.ShapeDtypeStruct((SHARE + EXTRA, WIDTH), BF16),
        scratch_shapes=[pltpu.SemaphoreType.DMA((4,))],
        name="pack",
    )(counts, embeddings, validity.reshape(16, GRANULE))


def add_share(query, row_bias, message_ref, total_ref, weighted_ref, own):
    extra = message_ref[SHARE:, :].astype(F32)
    half = SHARE // 2
    if own:
        offset = lax.broadcasted_iota(jnp.int32, (TILE, GRANULE), 0) - lax.broadcasted_iota(
            jnp.int32, (TILE, GRANULE), 1
        )
        shift = lax.axis_index("rep") * GRANULE
    for h in range(2):
        rows = message_ref[h * half : (h + 1) * half, :]
        bias = extra[h : h + 1] + extra[2 + h : 3 + h] + extra[4 + h : 5 + h]
        gram = lax.dot_general(query, rows, NT, preferred_element_type=F32)
        kernel = jnp.exp2(gram * CROSS + (row_bias + bias))
        if own:
            pieces = []
            for j in range(2):
                here = jnp.where(pl.program_id(0) == 2 * h + j, shift, SLOTS)
                piece = kernel[:, j * GRANULE : (j + 1) * GRANULE]
                pieces.append(jnp.where(offset == here, 0.0, piece))
            kernel = jnp.concatenate(pieces, 1)
        total_ref[...] += kernel[:, :GRANULE] + kernel[:, GRANULE:]
        weighted_ref[...] += jnp.dot(kernel.astype(BF16), rows, preferred_element_type=F32)


def query_bias(query):
    wide = query.astype(F32)
    return jnp.sum(wide * wide, axis=1, keepdims=True) * ROW


def first_body(query_ref, message_ref, total_ref, weighted_ref):
    query = query_ref[...]
    total_ref[...] = jnp.zeros_like(total_ref)
    weighted_ref[...] = jnp.zeros_like(weighted_ref)
    add_share(query, query_bias(query), message_ref, total_ref, weighted_ref, True)


def middle_body(query_ref, total_in, weighted_in, *refs):
    messages, (total_ref, weighted_ref) = refs[:-2], refs[-2:]
    query = query_ref[...]
    bias = query_bias(query)
    total_ref[...] = total_in[...]
    weighted_ref[...] = weighted_in[...]
    for message_ref in messages:
        add_share(query, bias, message_ref, total_ref, weighted_ref, False)


def last_body(query_ref, total_in, weighted_in, *refs):
    messages, (keep_ref, send_ref, total_ref, weighted_ref) = refs[:-4], refs[-4:]
    middle_body(query_ref, total_in, weighted_in, *messages, total_ref, weighted_ref)
    total = jnp.sum(total_ref[...].T, axis=0, keepdims=True)
    total = jnp.broadcast_to(total, (8, TILE))
    turned = weighted_ref[...].T
    core = lax.axis_index("rep") % 2
    quarter = [turned[PART * i : PART * (i + 1)] for i in range(4)]
    for part in range(2):
        first, second = quarter[2 * part], quarter[2 * part + 1]
        keep_ref[PART * part : PART * (part + 1), :] = jnp.where(core == 0, first, second)
        send_ref[PART * part : PART * (part + 1), :] = jnp.where(core == 0, second, first)
    keep_ref[2 * PART :, :] = total
    send_ref[2 * PART :, :] = total


def cost(shares):
    return pl.CostEstimate(
        flops=shares * 4 * SLOTS * SHARE * WIDTH,
        bytes_accessed=4 * SLOTS * (WIDTH + GRANULE) * 2,
        transcendentals=shares * SLOTS * SHARE,
    )


QUERY = pl.BlockSpec((TILE, WIDTH), lambda i: (i, 0))
TOTAL = pl.BlockSpec((TILE, GRANULE), lambda i: (i, 0))
MESSAGE = pl.BlockSpec((SHARE + EXTRA, WIDTH), lambda i: (0, 0))
SUMS = (
    jax.ShapeDtypeStruct((SLOTS, GRANULE), F32),
    jax.ShapeDtypeStruct((SLOTS, WIDTH), F32),
)
PARAMS = pltpu.CompilerParams(vmem_limit_bytes=VMEM_LIMIT)


def first(query, message):
    return pl.pallas_call(
        first_body,
        grid=(SLOTS // TILE,),
        in_specs=[QUERY, MESSAGE],
        out_specs=(TOTAL, QUERY),
        out_shape=SUMS,
        compiler_params=PARAMS,
        cost_estimate=cost(1),
        name="first",
    )(query, message)


def middle(query, sums, messages):
    return pl.pallas_call(
        middle_body,
        grid=(SLOTS // TILE,),
        in_specs=[QUERY, TOTAL, QUERY] + [MESSAGE] * len(messages),
        out_specs=(TOTAL, QUERY),
        out_shape=SUMS,
        compiler_params=PARAMS,
        cost_estimate=cost(len(messages)),
        name="middle",
    )(query, *sums, *messages)


def last(query, sums, messages):
    half = pl.BlockSpec((2 * PART + 8, TILE), lambda i: (0, i))
    shape = jax.ShapeDtypeStruct((2 * PART + 8, SLOTS), F32)
    return pl.pallas_call(
        last_body,
        grid=(SLOTS // TILE,),
        in_specs=[QUERY, TOTAL, QUERY] + [MESSAGE] * len(messages),
        out_specs=(half, half),
        out_shape=(shape, shape),
        scratch_shapes=[pltpu.VMEM((TILE, GRANULE), F32), pltpu.VMEM((TILE, WIDTH), F32)],
        compiler_params=PARAMS,
        cost_estimate=cost(len(messages)),
        name="last",
    )(query, *sums, *messages)


def join_body(keep_ref, came_ref, sum_ref, message_ref):
    chip = lax.axis_index("rep") // 2
    both = keep_ref[...] + came_ref[...]
    low, high = both[:PART], both[PART : 2 * PART]
    total = both[2 * PART :]
    sum_ref[:PART, :] = jnp.where(chip == 0, low, high)
    sum_ref[PART:, :] = total
    message_ref[:PART, :] = jnp.where(chip == 0, high, low).astype(BF16)
    parts = [part.astype(F32)[:1] for part in split3(total)]
    parts.append(jnp.zeros((EXTRA - 3, total.shape[1]), F32))
    message_ref[PART:, :] = jnp.concatenate(parts, 0).astype(BF16)


def join(keep, came):
    tile = 1024
    return pl.pallas_call(
        join_body,
        grid=(SLOTS // tile,),
        in_specs=[pl.BlockSpec((2 * PART + 8, tile), lambda i: (0, i))] * 2,
        out_specs=(
            pl.BlockSpec((PART + 8, tile), lambda i: (0, i)),
            pl.BlockSpec((PART + EXTRA, tile), lambda i: (0, i)),
        ),
        out_shape=(
            jax.ShapeDtypeStruct((PART + 8, SLOTS), F32),
            jax.ShapeDtypeStruct((PART + EXTRA, SLOTS), BF16),
        ),
        name="join",
    )(keep, came)


def finish_body(counts_ref, validity_ref, sum_ref, came_ref, log_ref, mean_ref):
    tile = sum_ref.shape[1]
    extra = came_ref[PART:, :].astype(F32)
    total = sum_ref[PART : PART + 1, :] + (extra[0:1] + extra[1:2] + extra[2:3])
    position = pl.program_id(0) * tile + lax.broadcasted_iota(jnp.int32, (1, tile), 1)
    live = ((position < counts_ref[0]) & (validity_ref[...] == 1)).astype(F32)
    shifted = total + EPSILON
    log_ref[...] = live * jnp.log(shifted)
    scale = live / shifted
    mean_ref[...] = (sum_ref[:PART, :] + came_ref[:PART, :].astype(F32)) * scale


def finish(counts, validity, summed, came):
    tile = 1024
    return pl.pallas_call(
        finish_body,
        grid=(SLOTS // tile,),
        in_specs=[
            pl.BlockSpec(memory_space=pltpu.SMEM),
            pl.BlockSpec((1, tile), lambda i: (0, i)),
            pl.BlockSpec((PART + 8, tile), lambda i: (0, i)),
            pl.BlockSpec((PART + EXTRA, tile), lambda i: (0, i)),
        ],
        out_specs=(
            pl.BlockSpec((1, tile), lambda i: (0, i)),
            pl.BlockSpec((PART, tile), lambda i: (0, i)),
        ),
        out_shape=(
            jax.ShapeDtypeStruct((1, SLOTS), F32),
            jax.ShapeDtypeStruct((PART, SLOTS), F32),
        ),
        name="finish",
    )(counts, validity.reshape(1, SLOTS), summed, came)


def route(blocks, reps, move):
    pairs = []
    for block in range(blocks):
        for rep in range(reps):
            row, column = divmod(block, 2)
            (row_to, column_to), rep_to = move(row, column, rep)
            block_to = (row_to * 2 + column_to) % blocks
            pairs.append((block * reps + rep, block_to * reps + rep_to))
    return pairs


def on_device(embeddings, counts, validity):
    blocks, reps = lax.axis_size("blk"), lax.axis_size("rep")

    def send(value, move):
        return lax.ppermute(value, ("blk", "rep"), route(blocks, reps, move))

    ahead = lambda m, h, r: ((m + 2 * h - 1, h), r)
    behind = lambda m, h, r: ((m + 1 - 2 * h, h), r)
    across = lambda m, h, r: ((m, 1 - h), r ^ 2)
    corner = lambda m, h, r: ((m + 2 * h - 1, 1 - h), r ^ 2)
    other_core = lambda m, h, r: ((m, h), r ^ 1)
    other_chip = lambda m, h, r: ((m, h), r ^ 2)

    mine = pack(embeddings, counts, validity)
    from_ahead = send(mine, ahead)
    from_across = send(mine, across)
    from_behind = send(mine, behind)
    sums = first(embeddings, mine)
    far = send(from_ahead, corner)
    side = send(from_ahead, across)
    near = send(from_across, ahead)
    sums = middle(embeddings, sums, (from_ahead, from_across, from_behind))
    keep, give = last(embeddings, sums, (far, side, near))
    summed, message = join(keep, send(give, other_core))
    log_density, mean = finish(counts, validity, summed, send(message, other_chip))
    return log_density.reshape(SLOTS), mean.T


def solution(mesh):
    return jax.shard_map(
        on_device,
        mesh=mesh,
        in_specs=(P("blk", None), P("blk"), P("blk")),
        out_specs=(P("blk"), P("blk", "rep")),
        check_vma=False,
    )
```

```python
import functools
import math

import jax
import jax.numpy as jnp
from jax import lax
from jax.experimental import pallas as pl
from jax.experimental.pallas import tpu as pltpu
from jax.sharding import PartitionSpec as P

BETA = 8.0
EPSILON = 1e-06
LOG2E = math.log2(math.e)
DEAD = -1e30

SLOTS = 2048
WIDTH = 256
SHARE = 512
GRANULE = 128
EXTRA = 8
TILE = 512
PART = 64
PIECES = 2

F32 = jnp.float32
BF16 = jnp.bfloat16
NT = (((1,), (1,)), ((), ()))
VMEM_LIMIT = 32 * 2**20

CROSS = 2.0 * BETA / WIDTH * LOG2E
ROW = -BETA / WIDTH * LOG2E
TOP = 2.0 * BETA * LOG2E


def split3(value):
    high = value.astype(BF16)
    rest = value - high.astype(F32)
    middle = rest.astype(BF16)
    low = (rest - middle.astype(F32)).astype(BF16)
    return high, middle, low


def pack_body(counts_ref, embeddings_ref, validity_ref, message_ref, count_ref, valid_ref, sems):
    rep = lax.axis_index("rep")
    copies = [
        pltpu.make_async_copy(
            embeddings_ref.at[pl.ds(pl.multiple_of((4 * k + rep) * GRANULE, GRANULE), GRANULE), :],
            message_ref.at[pl.ds(k * GRANULE, GRANULE), :],
            sems.at[k],
        )
        for k in range(4)
    ]
    copies.append(pltpu.make_async_copy(validity_ref, valid_ref, sems.at[4]))
    copies.append(pltpu.make_async_copy(counts_ref, count_ref, sems.at[5]))
    for copy in copies:
        copy.start()
    for copy in copies:
        copy.wait()
    rows = message_ref[:SHARE, :].astype(F32)
    square = rows * rows
    square = square[:, :GRANULE] + square[:, GRANULE:]
    norm = jnp.sum(square.T, axis=0, keepdims=True)
    biases = []
    for k in range(4):
        granule = 4 * k + rep
        position = granule * GRANULE + lax.broadcasted_iota(jnp.int32, (1, GRANULE), 1)
        live = (position < count_ref[0]) & (valid_ref[pl.ds(granule, 1), :] == 1)
        biases.append(jnp.where(live, TOP + ROW * norm[:, k * GRANULE : (k + 1) * GRANULE], DEAD))
    pairs = [jnp.concatenate(biases[:2], 1), jnp.concatenate(biases[2:], 1)]
    parts = [split3(pair) for pair in pairs]
    lines = [parts[h][level].astype(F32) for level in range(3) for h in range(2)]
    lines.append(jnp.zeros((EXTRA - 6, WIDTH), F32))
    message_ref[SHARE:, :] = jnp.concatenate(lines, 0).astype(BF16)


def pack(embeddings, counts, validity):
    return pl.pallas_call(
        pack_body,
        in_specs=[pl.BlockSpec(memory_space=pltpu.HBM)] * 3,
        out_specs=pl.BlockSpec(memory_space=pltpu.VMEM),
        out_shape=jax.ShapeDtypeStruct((SHARE + EXTRA, WIDTH), BF16),
        scratch_shapes=[
            pltpu.SMEM((1,), jnp.int32),
            pltpu.VMEM((SLOTS // GRANULE, GRANULE), jnp.int32),
            pltpu.SemaphoreType.DMA((6,)),
        ],
        compiler_params=pltpu.CompilerParams(vmem_limit_bytes=8 * 2**20),
        name="pack",
    )(counts, embeddings, validity.reshape(SLOTS // GRANULE, GRANULE))


def add_share(query, row_bias, message_ref, total_ref, weighted_ref, own):
    extra = message_ref[SHARE:, :].astype(F32)
    half = SHARE // 2
    if own:
        offset = lax.broadcasted_iota(jnp.int32, (TILE, GRANULE), 0) - lax.broadcasted_iota(
            jnp.int32, (TILE, GRANULE), 1
        )
        shift = lax.axis_index("rep") * GRANULE
    for h in range(2):
        rows = message_ref[h * half : (h + 1) * half, :]
        bias = extra[h : h + 1] + extra[2 + h : 3 + h] + extra[4 + h : 5 + h]
        gram = lax.dot_general(query, rows, NT, preferred_element_type=F32)
        kernel = jnp.exp2(gram * CROSS + (row_bias + bias))
        if own:
            pieces = []
            for j in range(2):
                here = jnp.where(pl.program_id(0) == 2 * h + j, shift, SLOTS)
                piece = kernel[:, j * GRANULE : (j + 1) * GRANULE]
                pieces.append(jnp.where(offset == here, 0.0, piece))
            kernel = jnp.concatenate(pieces, 1)
        total_ref[...] += kernel[:, :GRANULE] + kernel[:, GRANULE:]
        weighted_ref[...] += jnp.dot(kernel.astype(BF16), rows, preferred_element_type=F32)


def query_bias(query):
    wide = query.astype(F32)
    return jnp.sum(wide * wide, axis=1, keepdims=True) * ROW


def first_body(query_ref, message_ref, total_ref, weighted_ref):
    query = query_ref[...]
    total_ref[...] = jnp.zeros_like(total_ref)
    weighted_ref[...] = jnp.zeros_like(weighted_ref)
    add_share(query, query_bias(query), message_ref, total_ref, weighted_ref, True)


def middle_body(query_ref, total_in, weighted_in, *refs):
    messages, (total_ref, weighted_ref) = refs[:-2], refs[-2:]
    query = query_ref[...]
    bias = query_bias(query)
    total_ref[...] = total_in[...]
    weighted_ref[...] = weighted_in[...]
    for message_ref in messages:
        add_share(query, bias, message_ref, total_ref, weighted_ref, False)


def last_body(query_ref, total_in, weighted_in, *refs):
    messages, (keep_ref, send_ref, total_ref, weighted_ref) = refs[:-4], refs[-4:]
    middle_body(query_ref, total_in, weighted_in, *messages, total_ref, weighted_ref)
    total = jnp.sum(total_ref[...].T, axis=0, keepdims=True)
    total = jnp.broadcast_to(total, (8, TILE))
    turned = weighted_ref[...].T
    core = lax.axis_index("rep") % 2
    quarter = [turned[PART * i : PART * (i + 1)] for i in range(4)]
    for part in range(2):
        first, second = quarter[2 * part], quarter[2 * part + 1]
        keep_ref[PART * part : PART * (part + 1), :] = jnp.where(core == 0, first, second)
        send_ref[PART * part : PART * (part + 1), :] = jnp.where(core == 0, second, first)
    keep_ref[2 * PART :, :] = total
    send_ref[2 * PART :, :] = total


def cost(shares):
    return pl.CostEstimate(
        flops=int(shares * 4 * SLOTS * SHARE * WIDTH),
        bytes_accessed=4 * SLOTS * (WIDTH + GRANULE) * 2,
        transcendentals=int(shares * SLOTS * SHARE),
    )


QUERY = pl.BlockSpec((TILE, WIDTH), lambda i: (i, 0))
TOTAL = pl.BlockSpec((TILE, GRANULE), lambda i: (i, 0))
MESSAGE = pl.BlockSpec((SHARE + EXTRA, WIDTH), lambda i: (0, 0))
SUMS = (
    jax.ShapeDtypeStruct((SLOTS, GRANULE), F32),
    jax.ShapeDtypeStruct((SLOTS, WIDTH), F32),
)
PARAMS = pltpu.CompilerParams(vmem_limit_bytes=VMEM_LIMIT)
SMALL = pltpu.CompilerParams(vmem_limit_bytes=16 * 2**20)


def first(query, message):
    return pl.pallas_call(
        first_body,
        grid=(SLOTS // TILE,),
        in_specs=[QUERY, MESSAGE],
        out_specs=(TOTAL, QUERY),
        out_shape=SUMS,
        compiler_params=PARAMS,
        cost_estimate=cost(1),
        name="first",
    )(query, message)


def middle(query, sums, messages):
    return pl.pallas_call(
        middle_body,
        grid=(SLOTS // TILE,),
        in_specs=[QUERY, TOTAL, QUERY] + [MESSAGE] * len(messages),
        out_specs=(TOTAL, QUERY),
        out_shape=SUMS,
        compiler_params=PARAMS,
        cost_estimate=cost(len(messages)),
        name="middle",
    )(query, *sums, *messages)


def last(query, sums, messages, part):
    steps = SLOTS // TILE // PIECES
    rows = lambda width: pl.BlockSpec((TILE, width), lambda i: (i + steps * part, 0))
    half = pl.BlockSpec((2 * PART + 8, TILE), lambda i: (0, i))
    shape = jax.ShapeDtypeStruct((2 * PART + 8, SLOTS // PIECES), F32)
    return pl.pallas_call(
        last_body,
        grid=(steps,),
        in_specs=[rows(WIDTH), rows(GRANULE), rows(WIDTH)] + [MESSAGE] * len(messages),
        out_specs=(half, half),
        out_shape=(shape, shape),
        scratch_shapes=[pltpu.VMEM((TILE, GRANULE), F32), pltpu.VMEM((TILE, WIDTH), F32)],
        compiler_params=PARAMS,
        cost_estimate=cost(len(messages) / PIECES),
        name="last",
    )(query, *sums, *messages)


def join_body(keep_ref, came_ref, sum_ref, message_ref):
    chip = lax.axis_index("rep") // 2
    both = keep_ref[...] + came_ref[...]
    low, high = both[:PART], both[PART : 2 * PART]
    total = both[2 * PART :]
    sum_ref[:PART, :] = jnp.where(chip == 0, low, high)
    sum_ref[PART:, :] = total
    message_ref[:PART, :] = jnp.where(chip == 0, high, low).astype(BF16)
    parts = [part.astype(F32)[:1] for part in split3(total)]
    parts.append(jnp.zeros((EXTRA - 3, total.shape[1]), F32))
    message_ref[PART:, :] = jnp.concatenate(parts, 0).astype(BF16)


def join(keep, came):
    return pl.pallas_call(
        join_body,
        in_specs=[pl.BlockSpec(memory_space=pltpu.VMEM)] * 2,
        out_specs=[pl.BlockSpec(memory_space=pltpu.VMEM)] * 2,
        out_shape=(
            jax.ShapeDtypeStruct((PART + 8, SLOTS // PIECES), F32),
            jax.ShapeDtypeStruct((PART + EXTRA, SLOTS // PIECES), BF16),
        ),
        compiler_params=SMALL,
        cost_estimate=pl.CostEstimate(flops=10**6, bytes_accessed=3 * 10**6, transcendentals=0),
        name="join",
    )(keep, came)


def finish_body(counts_ref, validity_ref, *refs):
    halves, (log_ref, mean_ref) = refs[:-2], refs[-2:]
    tile = SLOTS // PIECES
    for part in range(PIECES):
        sum_ref, came_ref = halves[2 * part : 2 * part + 2]
        columns = slice(part * tile, (part + 1) * tile)
        extra = came_ref[PART:, :].astype(F32)
        total = sum_ref[PART : PART + 1, :] + (extra[0:1] + extra[1:2] + extra[2:3])
        position = part * tile + lax.broadcasted_iota(jnp.int32, (1, tile), 1)
        live = ((position < counts_ref[0]) & (validity_ref[:, columns] == 1)).astype(F32)
        shifted = total + EPSILON
        log_ref[:, columns] = live * jnp.log(shifted)
        scale = live / shifted
        mean_ref[:, columns] = (sum_ref[:PART, :] + came_ref[:PART, :].astype(F32)) * scale


def finish(counts, validity, halves):
    vmem = pl.BlockSpec(memory_space=pltpu.VMEM)
    return pl.pallas_call(
        finish_body,
        in_specs=[pl.BlockSpec(memory_space=pltpu.SMEM), vmem] + [vmem] * (2 * PIECES),
        out_specs=(vmem, vmem),
        out_shape=(
            jax.ShapeDtypeStruct((1, SLOTS), F32),
            jax.ShapeDtypeStruct((PART, SLOTS), F32),
        ),
        compiler_params=SMALL,
        name="finish",
    )(counts, validity.reshape(1, SLOTS), *halves)


def route(blocks, reps, move):
    pairs = []
    for block in range(blocks):
        for rep in range(reps):
            row, column = divmod(block, 2)
            (row_to, column_to), rep_to = move(row, column, rep)
            block_to = (row_to * 2 + column_to) % blocks
            pairs.append((block * reps + rep, block_to * reps + rep_to))
    return pairs


def on_device(embeddings, counts, validity):
    blocks, reps = lax.axis_size("blk"), lax.axis_size("rep")

    def send(value, move):
        return lax.ppermute(value, ("blk", "rep"), route(blocks, reps, move))

    ahead = lambda m, h, r: ((m + 2 * h - 1, h), r)
    behind = lambda m, h, r: ((m + 1 - 2 * h, h), r)
    across = lambda m, h, r: ((m, 1 - h), r ^ 2)
    corner = lambda m, h, r: ((m + 2 * h - 1, 1 - h), r ^ 2)
    other_core = lambda m, h, r: ((m, h), r ^ 1)
    other_chip = lambda m, h, r: ((m, h), r ^ 2)

    mine = pack(embeddings, counts, validity)
    from_ahead = send(mine, ahead)
    from_across = send(mine, across)
    from_behind = send(mine, behind)
    sums = first(embeddings, mine)
    far = send(from_ahead, corner)
    side = send(from_ahead, across)
    near = send(from_across, ahead)
    sums = middle(embeddings, sums, (from_ahead, from_across, from_behind))
    halves = []
    for part in range(PIECES):
        keep, give = last(embeddings, sums, (far, side, near), part)
        summed, message = join(keep, send(give, other_core))
        halves += [summed, send(message, other_chip)]
    log_density, mean = finish(counts, validity, halves)
    return log_density.reshape(SLOTS), mean.T


def solution(mesh):
    return jax.shard_map(
        on_device,
        mesh=mesh,
        in_specs=(P("blk", None), P("blk"), P("blk")),
        out_specs=(P("blk"), P("blk", "rep")),
        check_vma=False,
    )
```

```python
import functools
import math

import jax
import jax.numpy as jnp
from jax import lax
from jax.experimental import pallas as pl
from jax.experimental.pallas import tpu as pltpu
from jax.sharding import PartitionSpec as P

BETA = 8.0
EPSILON = 1e-06
LOG2E = math.log2(math.e)
DEAD = -1e30

SLOTS = 2048
WIDTH = 256
SHARE = 512
GRANULE = 128
EXTRA = 8
TILE = 512
PART = 64
PIECES = 2

F32 = jnp.float32
BF16 = jnp.bfloat16
NT = (((1,), (1,)), ((), ()))
VMEM_LIMIT = 32 * 2**20

CROSS = 2.0 * BETA / WIDTH * LOG2E
ROW = -BETA / WIDTH * LOG2E
TOP = 2.0 * BETA * LOG2E


def split3(value):
    high = value.astype(BF16)
    rest = value - high.astype(F32)
    middle = rest.astype(BF16)
    low = (rest - middle.astype(F32)).astype(BF16)
    return high, middle, low


def own_turn():
    return (lax.axis_index("rep") + lax.axis_index("blk")) % 4


def pack_body(counts_ref, embeddings_ref, validity_ref, message_ref, live_ref, count_ref, sems):
    turn = own_turn()
    copies = [
        pltpu.make_async_copy(
            embeddings_ref.at[pl.ds(pl.multiple_of((4 * k + turn) * GRANULE, GRANULE), GRANULE), :],
            message_ref.at[pl.ds(k * GRANULE, GRANULE), :],
            sems.at[k],
        )
        for k in range(4)
    ]
    copies.append(pltpu.make_async_copy(counts_ref, count_ref, sems.at[4]))
    copies.append(pltpu.make_async_copy(validity_ref, live_ref, sems.at[5]))
    for copy in copies:
        copy.start()
    for copy in copies:
        copy.wait()
    rows = message_ref[:SHARE, :].astype(F32)
    square = rows * rows
    square = square[:, :GRANULE] + square[:, GRANULE:]
    norm = jnp.sum(square.T, axis=0, keepdims=True)
    shape = (SLOTS // GRANULE, GRANULE)
    position = lax.broadcasted_iota(jnp.int32, shape, 0) * GRANULE
    position = position + lax.broadcasted_iota(jnp.int32, shape, 1)
    live_ref[...] = jnp.where((position < count_ref[0]) & (live_ref[...] == 1), 1, 0)
    biases = []
    for k in range(4):
        live = live_ref[pl.ds(4 * k + turn, 1), :] == 1
        biases.append(jnp.where(live, TOP + ROW * norm[:, k * GRANULE : (k + 1) * GRANULE], DEAD))
    pairs = [jnp.concatenate(biases[:2], 1), jnp.concatenate(biases[2:], 1)]
    parts = [split3(pair) for pair in pairs]
    lines = [parts[h][level].astype(F32) for level in range(3) for h in range(2)]
    filled = jnp.clip((count_ref[0] // GRANULE - turn + 3) // 4, 0, 4)
    lines.append(jnp.full((EXTRA - 6, WIDTH), filled.astype(F32)))
    message_ref[SHARE:, :] = jnp.concatenate(lines, 0).astype(BF16)


def pack(counts, embeddings, validity):
    vmem = pl.BlockSpec(memory_space=pltpu.VMEM)
    return pl.pallas_call(
        pack_body,
        in_specs=[pl.BlockSpec(memory_space=pl.ANY)] * 3,
        out_specs=(vmem, vmem),
        out_shape=(
            jax.ShapeDtypeStruct((SHARE + EXTRA, WIDTH), BF16),
            jax.ShapeDtypeStruct((SLOTS // GRANULE, GRANULE), jnp.int32),
        ),
        scratch_shapes=[pltpu.SMEM((1,), jnp.int32), pltpu.SemaphoreType.DMA((6,))],
        compiler_params=pltpu.CompilerParams(vmem_limit_bytes=53 * 2**20),
        name="pack",
    )(counts, embeddings, validity.reshape(SLOTS // GRANULE, GRANULE))


def query_bias(query):
    wide = query.astype(F32)
    return jnp.sum(wide * wide, axis=1, keepdims=True) * ROW


def first_body(query_ref, message_ref, total_ref, weighted_ref, bias_ref):
    query = query_ref[...]
    row_bias = jnp.broadcast_to(query_bias(query), (TILE, GRANULE))
    bias_ref[...] = row_bias
    row_bias = jnp.concatenate([row_bias, row_bias], 1)
    extra = message_ref[SHARE:, :].astype(F32)
    half = SHARE // 2
    shape = (TILE, GRANULE)
    offset = lax.broadcasted_iota(jnp.int32, shape, 0) - lax.broadcasted_iota(jnp.int32, shape, 1)
    shift = own_turn() * GRANULE
    for h in range(2):
        rows = message_ref[h * half : (h + 1) * half, :]
        bias = extra[h : h + 1] + extra[2 + h : 3 + h] + extra[4 + h : 5 + h]
        gram = lax.dot_general(query, rows, NT, preferred_element_type=F32)
        kernel = jnp.exp2(gram * CROSS + (row_bias + bias))
        pieces = []
        for j in range(2):
            here = jnp.where(pl.program_id(0) == 2 * h + j, shift, SLOTS)
            piece = kernel[:, j * GRANULE : (j + 1) * GRANULE]
            pieces.append(jnp.where(offset == here, 0.0, piece))
        kernel = jnp.concatenate(pieces, 1)
        total = pieces[0] + pieces[1]
        weighted = jnp.dot(kernel.astype(BF16), rows, preferred_element_type=F32)
        if h == 0:
            total_ref[...] = total
            weighted_ref[...] = weighted
        else:
            total_ref[...] += total
            weighted_ref[...] += weighted


def collect(messages, rows_ref, cols_ref):
    rows_ref[...] = jnp.zeros_like(rows_ref)
    cols_ref[...] = jnp.full_like(cols_ref, DEAD)
    place = jnp.int32(0)
    for message_ref in messages:
        extra = message_ref[SHARE:, :].astype(F32)
        filled = jnp.max(extra[6:7]).astype(jnp.int32)
        for k in range(4):
            start = pl.multiple_of((place + k) * GRANULE, GRANULE)
            rows_ref[pl.ds(start, GRANULE), :] = message_ref[k * GRANULE : (k + 1) * GRANULE, :]
            h, lanes = k // 2, slice((k % 2) * GRANULE, (k % 2 + 1) * GRANULE)
            bias = extra[h : h + 1, lanes] + extra[2 + h : 3 + h, lanes] + extra[4 + h : 5 + h, lanes]
            cols_ref[pl.ds(place + k, 1), :] = bias
        place = place + filled
    return (place + 1) // 2


def accumulate(pairs, base, chunks, query_ref, bias_ref, rows_ref, cols_ref, total_ref, weighted_ref):
    def run(begin, count):
        for i in range(count):
            pair = begin + i
            start = pl.multiple_of(pair * 2 * GRANULE, 2 * GRANULE)
            rows = rows_ref[pl.ds(start, 2 * GRANULE), :]
            bias = [cols_ref[pl.ds(2 * pair + j, 1), :] for j in range(2)]
            bias = jnp.concatenate(bias, 1)
            for chunk in range(chunks):
                here = slice(base + chunk * TILE, base + (chunk + 1) * TILE)
                there = slice(chunk * TILE, (chunk + 1) * TILE)
                row_bias = bias_ref[here, :]
                row_bias = jnp.concatenate([row_bias, row_bias], 1)
                gram = lax.dot_general(query_ref[here, :], rows, NT, preferred_element_type=F32)
                kernel = jnp.exp2(gram * CROSS + (row_bias + bias))
                total_ref[there, :] += kernel[:, :GRANULE] + kernel[:, GRANULE:]
                weighted_ref[there, :] += jnp.dot(
                    kernel.astype(BF16), rows, preferred_element_type=F32
                )

    done = jnp.int32(0)
    for count in (4, 2, 1):
        fits = pairs - done >= count
        pl.when(fits)(functools.partial(run, done, count))
        done = done + jnp.where(fits, count, 0)


def middle_body(shares, query_ref, bias_ref, total_in, weighted_in, *refs):
    messages, (total_ref, weighted_ref, rows_ref, cols_ref) = refs[:shares], refs[shares:]
    pairs = collect(messages, rows_ref, cols_ref)
    accumulate(
        pairs, 0, SLOTS // TILE, query_ref, bias_ref, rows_ref, cols_ref, total_ref, weighted_ref
    )


def last_body(shares, part, query_ref, bias_ref, total_in, weighted_in, *refs):
    messages = refs[:shares]
    keep_ref, send_ref, rows_ref, cols_ref, total_ref, weighted_ref = refs[shares:]
    size = SLOTS // PIECES
    base = part * size
    total_ref[...] = total_in[base : base + size, :]
    weighted_ref[...] = weighted_in[base : base + size, :]
    pairs = collect(messages, rows_ref, cols_ref)
    accumulate(
        pairs, base, size // TILE, query_ref, bias_ref, rows_ref, cols_ref, total_ref, weighted_ref
    )
    core = lax.axis_index("rep") % 2
    for tile in range(size // TILE):
        here = slice(tile * TILE, (tile + 1) * TILE)
        total = jnp.sum(total_ref[here, :].T, axis=0, keepdims=True)
        total = jnp.broadcast_to(total, (8, TILE))
        turned = weighted_ref[here, :].T
        quarter = [turned[PART * i : PART * (i + 1)] for i in range(4)]
        for half in range(2):
            first, second = quarter[2 * half], quarter[2 * half + 1]
            keep_ref[PART * half : PART * (half + 1), here] = jnp.where(core == 0, first, second)
            send_ref[PART * half : PART * (half + 1), here] = jnp.where(core == 0, second, first)
        keep_ref[2 * PART :, here] = total
        send_ref[2 * PART :, here] = total


def cost(shares):
    return pl.CostEstimate(
        flops=int(shares * 4 * SLOTS * SHARE * WIDTH),
        bytes_accessed=4 * SLOTS * (WIDTH + GRANULE) * 2,
        transcendentals=int(shares * SLOTS * SHARE),
    )


WHOLE = pl.BlockSpec(memory_space=pltpu.VMEM)
QUERY = pl.BlockSpec((TILE, WIDTH), lambda i: (i, 0))
TOTAL = pl.BlockSpec((TILE, GRANULE), lambda i: (i, 0))
MESSAGE = pl.BlockSpec((SHARE + EXTRA, WIDTH), lambda i: (0, 0))
SUMS = (
    jax.ShapeDtypeStruct((SLOTS, GRANULE), F32),
    jax.ShapeDtypeStruct((SLOTS, WIDTH), F32),
)
PARAMS = pltpu.CompilerParams(vmem_limit_bytes=VMEM_LIMIT)
SMALL = pltpu.CompilerParams(vmem_limit_bytes=16 * 2**20)


def first(query, message):
    return pl.pallas_call(
        first_body,
        grid=(SLOTS // TILE,),
        in_specs=[QUERY, MESSAGE],
        out_specs=(TOTAL, QUERY, TOTAL),
        out_shape=SUMS + (jax.ShapeDtypeStruct((SLOTS, GRANULE), F32),),
        compiler_params=PARAMS,
        cost_estimate=cost(1),
        name="first",
    )(query, message)


def line_up(shares):
    return [
        pltpu.VMEM((4 * shares * GRANULE, WIDTH), BF16),
        pltpu.VMEM((4 * shares, GRANULE), F32),
    ]


def middle(query, bias, sums, messages):
    shares = len(messages)
    return pl.pallas_call(
        functools.partial(middle_body, shares),
        in_specs=[WHOLE] * (4 + shares),
        out_specs=(WHOLE, WHOLE),
        out_shape=SUMS,
        scratch_shapes=line_up(shares),
        input_output_aliases={2: 0, 3: 1},
        compiler_params=PARAMS,
        cost_estimate=cost(shares),
        name="middle",
    )(query, bias, *sums, *messages)


def last(query, bias, sums, messages, part):
    shares = len(messages)
    size = SLOTS // PIECES
    shape = jax.ShapeDtypeStruct((2 * PART + 8, size), F32)
    return pl.pallas_call(
        functools.partial(last_body, shares, part),
        in_specs=[WHOLE] * (4 + shares),
        out_specs=(WHOLE, WHOLE),
        out_shape=(shape, shape),
        scratch_shapes=line_up(shares)
        + [pltpu.VMEM((size, GRANULE), F32), pltpu.VMEM((size, WIDTH), F32)],
        compiler_params=PARAMS,
        cost_estimate=cost(shares / PIECES),
        name="last",
    )(query, bias, *sums, *messages)


def join_body(keep_ref, came_ref, sum_ref, message_ref):
    chip = lax.axis_index("rep") // 2
    both = keep_ref[...] + came_ref[...]
    low, high = both[:PART], both[PART : 2 * PART]
    total = both[2 * PART :]
    sum_ref[:PART, :] = jnp.where(chip == 0, low, high)
    sum_ref[PART:, :] = total
    message_ref[:PART, :] = jnp.where(chip == 0, high, low).astype(BF16)
    parts = [part.astype(F32)[:1] for part in split3(total)]
    parts.append(jnp.zeros((EXTRA - 3, total.shape[1]), F32))
    message_ref[PART:, :] = jnp.concatenate(parts, 0).astype(BF16)


def join(keep, came):
    return pl.pallas_call(
        join_body,
        in_specs=[pl.BlockSpec(memory_space=pltpu.VMEM)] * 2,
        out_specs=[pl.BlockSpec(memory_space=pltpu.VMEM)] * 2,
        out_shape=(
            jax.ShapeDtypeStruct((PART + 8, SLOTS // PIECES), F32),
            jax.ShapeDtypeStruct((PART + EXTRA, SLOTS // PIECES), BF16),
        ),
        compiler_params=SMALL,
        cost_estimate=pl.CostEstimate(flops=10**6, bytes_accessed=3 * 10**6, transcendentals=0),
        name="join",
    )(keep, came)


def finish_body(live_ref, *refs):
    halves, (log_ref, mean_ref) = refs[:-2], refs[-2:]
    tile = SLOTS // PIECES
    for part in range(PIECES):
        sum_ref, came_ref = halves[2 * part : 2 * part + 2]
        columns = slice(part * tile, (part + 1) * tile)
        extra = came_ref[PART:, :].astype(F32)
        total = sum_ref[PART : PART + 1, :] + (extra[0:1] + extra[1:2] + extra[2:3])
        live = live_ref[:, columns].astype(F32)
        shifted = total + EPSILON
        log_ref[:, columns] = live * jnp.log(shifted)
        scale = live / shifted
        mean_ref[:, columns] = (sum_ref[:PART, :] + came_ref[:PART, :].astype(F32)) * scale


def finish(live, halves):
    vmem = pl.BlockSpec(memory_space=pltpu.VMEM)
    return pl.pallas_call(
        finish_body,
        in_specs=[vmem] * (1 + 2 * PIECES),
        out_specs=(vmem, vmem),
        out_shape=(
            jax.ShapeDtypeStruct((1, SLOTS), F32),
            jax.ShapeDtypeStruct((PART, SLOTS), F32),
        ),
        compiler_params=SMALL,
        name="finish",
    )(live.reshape(1, SLOTS), *halves)


def route(blocks, reps, move):
    pairs = []
    for block in range(blocks):
        for rep in range(reps):
            row, column = divmod(block, 2)
            (row_to, column_to), rep_to = move(row, column, rep)
            block_to = (row_to * 2 + column_to) % blocks
            pairs.append((block * reps + rep, block_to * reps + rep_to))
    return pairs


def on_device(embeddings, counts, validity):
    blocks, reps = lax.axis_size("blk"), lax.axis_size("rep")

    def send(value, move):
        return lax.ppermute(value, ("blk", "rep"), route(blocks, reps, move))

    ahead = lambda m, h, r: ((m + 2 * h - 1, h), r)
    behind = lambda m, h, r: ((m + 1 - 2 * h, h), r)
    across = lambda m, h, r: ((m, 1 - h), r ^ 2)
    corner = lambda m, h, r: ((m + 2 * h - 1, 1 - h), r ^ 2)
    other_core = lambda m, h, r: ((m, h), r ^ 1)
    other_chip = lambda m, h, r: ((m, h), r ^ 2)

    mine, live = pack(counts, embeddings, validity)
    from_across = send(mine, across)
    from_ahead = send(mine, ahead)
    from_behind = send(mine, behind)
    *sums, bias = first(embeddings, mine)
    far = send(from_ahead, corner)
    side = send(from_ahead, across)
    near = send(from_across, ahead)
    sums = middle(embeddings, bias, sums, (from_across, from_ahead, from_behind))
    sums = middle(embeddings, bias, sums, (far,))
    halves = []
    for part in range(PIECES):
        keep, give = last(embeddings, bias, sums, (side, near), part)
        summed, message = join(keep, send(give, other_core))
        halves += [summed, send(message, other_chip)]
    log_density, mean = finish(live, halves)
    return log_density.reshape(SLOTS), mean.T


def solution(mesh):
    return jax.shard_map(
        on_device,
        mesh=mesh,
        in_specs=(P("blk", None), P("blk"), P("blk")),
        out_specs=(P("blk"), P("blk", "rep")),
        check_vma=False,
    )
```

```python
import functools
import math

import jax
import jax.numpy as jnp
from jax import lax
from jax.experimental import pallas as pl
from jax.experimental.pallas import tpu as pltpu
from jax.sharding import PartitionSpec as P

BETA = 8.0
EPSILON = 1e-06
LOG2E = math.log2(math.e)
DEAD = -1e30

SLOTS = 2048
WIDTH = 256
SHARE = 512
GRANULE = 128
EXTRA = 8
TILE = 512
PART = 64
PIECES = (1280, 768)

F32 = jnp.float32
BF16 = jnp.bfloat16
NT = (((1,), (1,)), ((), ()))
VMEM_LIMIT = 32 * 2**20

CROSS = 2.0 * BETA / WIDTH * LOG2E
ROW = -BETA / WIDTH * LOG2E
TOP = 2.0 * BETA * LOG2E


def split3(value):
    high = value.astype(BF16)
    rest = value - high.astype(F32)
    middle = rest.astype(BF16)
    low = (rest - middle.astype(F32)).astype(BF16)
    return high, middle, low


def own_turn():
    return (lax.axis_index("rep") + lax.axis_index("blk")) % 4


def pack_body(counts_ref, embeddings_ref, validity_ref, message_ref, live_ref, count_ref, sems):
    turn = own_turn()
    copies = [
        pltpu.make_async_copy(
            embeddings_ref.at[pl.ds(pl.multiple_of((4 * k + turn) * GRANULE, GRANULE), GRANULE), :],
            message_ref.at[pl.ds(k * GRANULE, GRANULE), :],
            sems.at[k],
        )
        for k in range(4)
    ]
    copies.append(pltpu.make_async_copy(counts_ref, count_ref, sems.at[4]))
    copies.append(pltpu.make_async_copy(validity_ref, live_ref, sems.at[5]))
    for copy in copies:
        copy.start()
    for copy in copies:
        copy.wait()
    rows = message_ref[:SHARE, :].astype(F32)
    square = rows * rows
    square = square[:, :GRANULE] + square[:, GRANULE:]
    norm = jnp.sum(square.T, axis=0, keepdims=True)
    shape = (SLOTS // GRANULE, GRANULE)
    position = lax.broadcasted_iota(jnp.int32, shape, 0) * GRANULE
    position = position + lax.broadcasted_iota(jnp.int32, shape, 1)
    live_ref[...] = jnp.where((position < count_ref[0]) & (live_ref[...] == 1), 1, 0)
    biases = []
    for k in range(4):
        live = live_ref[pl.ds(4 * k + turn, 1), :] == 1
        biases.append(jnp.where(live, TOP + ROW * norm[:, k * GRANULE : (k + 1) * GRANULE], DEAD))
    pairs = [jnp.concatenate(biases[:2], 1), jnp.concatenate(biases[2:], 1)]
    parts = [split3(pair) for pair in pairs]
    lines = [parts[h][level].astype(F32) for level in range(3) for h in range(2)]
    filled = jnp.clip((count_ref[0] // GRANULE - turn + 3) // 4, 0, 4)
    lines.append(jnp.full((EXTRA - 6, WIDTH), filled.astype(F32)))
    message_ref[SHARE:, :] = jnp.concatenate(lines, 0).astype(BF16)


def pack(counts, embeddings, validity):
    vmem = pl.BlockSpec(memory_space=pltpu.VMEM)
    return pl.pallas_call(
        pack_body,
        in_specs=[pl.BlockSpec(memory_space=pl.ANY)] * 3,
        out_specs=(vmem, vmem),
        out_shape=(
            jax.ShapeDtypeStruct((SHARE + EXTRA, WIDTH), BF16),
            jax.ShapeDtypeStruct((SLOTS // GRANULE, GRANULE), jnp.int32),
        ),
        scratch_shapes=[pltpu.SMEM((1,), jnp.int32), pltpu.SemaphoreType.DMA((6,))],
        compiler_params=pltpu.CompilerParams(vmem_limit_bytes=53 * 2**20),
        name="pack",
    )(counts, embeddings, validity.reshape(SLOTS // GRANULE, GRANULE))


def query_bias(query):
    wide = query.astype(F32)
    return jnp.sum(wide * wide, axis=1, keepdims=True) * ROW


def first_body(query_ref, message_ref, total_ref, weighted_ref, bias_ref):
    query = query_ref[...]
    row_bias = jnp.broadcast_to(query_bias(query), (TILE, GRANULE))
    bias_ref[...] = row_bias
    row_bias = jnp.concatenate([row_bias, row_bias], 1)
    extra = message_ref[SHARE:, :].astype(F32)
    half = SHARE // 2
    shape = (TILE, GRANULE)
    offset = lax.broadcasted_iota(jnp.int32, shape, 0) - lax.broadcasted_iota(jnp.int32, shape, 1)
    shift = own_turn() * GRANULE
    for h in range(2):
        rows = message_ref[h * half : (h + 1) * half, :]
        bias = extra[h : h + 1] + extra[2 + h : 3 + h] + extra[4 + h : 5 + h]
        gram = lax.dot_general(query, rows, NT, preferred_element_type=F32)
        kernel = jnp.exp2(gram * CROSS + (row_bias + bias))
        pieces = []
        for j in range(2):
            here = jnp.where(pl.program_id(0) == 2 * h + j, shift, SLOTS)
            piece = kernel[:, j * GRANULE : (j + 1) * GRANULE]
            pieces.append(jnp.where(offset == here, 0.0, piece))
        kernel = jnp.concatenate(pieces, 1)
        total = pieces[0] + pieces[1]
        weighted = jnp.dot(kernel.astype(BF16), rows, preferred_element_type=F32)
        if h == 0:
            total_ref[...] = total
            weighted_ref[...] = weighted
        else:
            total_ref[...] += total
            weighted_ref[...] += weighted


def cut(begin, size):
    step = TILE if size % TILE == 0 else size // 2
    return [slice(at, at + step) for at in range(begin, begin + size, step)]


def collect(messages, rows_ref, cols_ref):
    rows_ref[...] = jnp.zeros_like(rows_ref)
    cols_ref[...] = jnp.full_like(cols_ref, DEAD)
    place = jnp.int32(0)
    for message_ref in messages:
        extra = message_ref[SHARE:, :].astype(F32)
        filled = jnp.max(extra[6:7]).astype(jnp.int32)
        for k in range(4):
            start = pl.multiple_of((place + k) * GRANULE, GRANULE)
            rows_ref[pl.ds(start, GRANULE), :] = message_ref[k * GRANULE : (k + 1) * GRANULE, :]
            h, lanes = k // 2, slice((k % 2) * GRANULE, (k % 2 + 1) * GRANULE)
            bias = extra[h : h + 1, lanes] + extra[2 + h : 3 + h, lanes] + extra[4 + h : 5 + h, lanes]
            cols_ref[pl.ds(place + k, 1), :] = bias
        place = place + filled
    return (place + 1) // 2


def accumulate(pairs, chunks, base, query_ref, bias_ref, rows_ref, cols_ref, total_ref, weighted_ref):
    def run(begin, count):
        for i in range(count):
            pair = begin + i
            start = pl.multiple_of(pair * 2 * GRANULE, 2 * GRANULE)
            rows = rows_ref[pl.ds(start, 2 * GRANULE), :]
            bias = [cols_ref[pl.ds(2 * pair + j, 1), :] for j in range(2)]
            bias = jnp.concatenate(bias, 1)
            for here in chunks:
                there = slice(here.start - base, here.stop - base)
                row_bias = bias_ref[here, :]
                row_bias = jnp.concatenate([row_bias, row_bias], 1)
                gram = lax.dot_general(query_ref[here, :], rows, NT, preferred_element_type=F32)
                kernel = jnp.exp2(gram * CROSS + (row_bias + bias))
                total_ref[there, :] += kernel[:, :GRANULE] + kernel[:, GRANULE:]
                weighted_ref[there, :] += jnp.dot(
                    kernel.astype(BF16), rows, preferred_element_type=F32
                )

    done = jnp.int32(0)
    for count in (4, 2, 1):
        fits = pairs - done >= count
        pl.when(fits)(functools.partial(run, done, count))
        done = done + jnp.where(fits, count, 0)


def middle_body(shares, query_ref, bias_ref, total_in, weighted_in, *refs):
    messages, (total_ref, weighted_ref, rows_ref, cols_ref) = refs[:shares], refs[shares:]
    pairs = collect(messages, rows_ref, cols_ref)
    chunks = cut(0, SLOTS)
    accumulate(pairs, chunks, 0, query_ref, bias_ref, rows_ref, cols_ref, total_ref, weighted_ref)


def last_body(shares, begin, size, query_ref, bias_ref, total_in, weighted_in, *refs):
    messages = refs[:shares]
    keep_ref, send_ref, rows_ref, cols_ref, total_ref, weighted_ref = refs[shares:]
    whole = slice(begin, begin + size)
    total_ref[...] = total_in[whole, :]
    weighted_ref[...] = weighted_in[whole, :]
    pairs = collect(messages, rows_ref, cols_ref)
    chunks = cut(begin, size)
    accumulate(
        pairs, chunks, begin, query_ref, bias_ref, rows_ref, cols_ref, total_ref, weighted_ref
    )
    core = lax.axis_index("rep") % 2
    for here in chunks:
        there = slice(here.start - begin, here.stop - begin)
        total = jnp.sum(total_ref[there, :].T, axis=0, keepdims=True)
        total = jnp.broadcast_to(total, (8, total.shape[1]))
        turned = weighted_ref[there, :].T
        quarter = [turned[PART * i : PART * (i + 1)] for i in range(4)]
        for half in range(2):
            first, second = quarter[2 * half], quarter[2 * half + 1]
            keep_ref[PART * half : PART * (half + 1), there] = jnp.where(core == 0, first, second)
            send_ref[PART * half : PART * (half + 1), there] = jnp.where(core == 0, second, first)
        keep_ref[2 * PART :, there] = total
        send_ref[2 * PART :, there] = total


def cost(shares):
    return pl.CostEstimate(
        flops=int(shares * 4 * SLOTS * SHARE * WIDTH),
        bytes_accessed=4 * SLOTS * (WIDTH + GRANULE) * 2,
        transcendentals=int(shares * SLOTS * SHARE),
    )


WHOLE = pl.BlockSpec(memory_space=pltpu.VMEM)
QUERY = pl.BlockSpec((TILE, WIDTH), lambda i: (i, 0))
TOTAL = pl.BlockSpec((TILE, GRANULE), lambda i: (i, 0))
MESSAGE = pl.BlockSpec((SHARE + EXTRA, WIDTH), lambda i: (0, 0))
SUMS = (
    jax.ShapeDtypeStruct((SLOTS, GRANULE), F32),
    jax.ShapeDtypeStruct((SLOTS, WIDTH), F32),
)
PARAMS = pltpu.CompilerParams(vmem_limit_bytes=VMEM_LIMIT)
SMALL = pltpu.CompilerParams(vmem_limit_bytes=16 * 2**20)


def first(query, message):
    return pl.pallas_call(
        first_body,
        grid=(SLOTS // TILE,),
        in_specs=[QUERY, MESSAGE],
        out_specs=(TOTAL, QUERY, TOTAL),
        out_shape=SUMS + (jax.ShapeDtypeStruct((SLOTS, GRANULE), F32),),
        compiler_params=PARAMS,
        cost_estimate=cost(1),
        name="first",
    )(query, message)


def line_up(shares):
    return [((4 * shares * GRANULE, WIDTH), BF16), ((4 * shares, GRANULE), F32)]


def middle(query, bias, sums, messages):
    shares = len(messages)
    return pl.pallas_call(
        functools.partial(middle_body, shares),
        in_specs=[WHOLE] * (4 + shares),
        out_specs=(WHOLE, WHOLE),
        out_shape=SUMS,
        scratch_shapes=[pltpu.VMEM(*spec) for spec in line_up(shares)],
        input_output_aliases={2: 0, 3: 1},
        compiler_params=PARAMS,
        cost_estimate=cost(shares),
        name="middle",
    )(query, bias, *sums, *messages)


def last(query, bias, sums, messages, begin, size):
    shares = len(messages)
    shape = jax.ShapeDtypeStruct((2 * PART + 8, size), F32)
    scratch = line_up(shares) + [((size, GRANULE), F32), ((size, WIDTH), F32)]
    return pl.pallas_call(
        functools.partial(last_body, shares, begin, size),
        in_specs=[WHOLE] * (4 + shares),
        out_specs=(WHOLE, WHOLE),
        out_shape=(shape, shape),
        scratch_shapes=[pltpu.VMEM(*spec) for spec in scratch],
        compiler_params=PARAMS,
        cost_estimate=cost(len(messages) * size / SLOTS),
        name="last",
    )(query, bias, *sums, *messages)


def join_body(keep_ref, came_ref, *refs):
    *before, sum_ref, message_ref = refs
    size = keep_ref.shape[1]
    chip = lax.axis_index("rep") // 2
    both = keep_ref[...] + came_ref[...]
    low, high = both[:PART], both[PART : 2 * PART]
    total = both[2 * PART :]
    sum_ref[:PART, :] = jnp.where(chip == 0, low, high)
    sum_ref[PART:, :] = total
    message_ref[:, :size] = jnp.where(chip == 0, high, low).astype(BF16)
    if message_ref.shape[1] > size:
        totals = [ref[PART : PART + 1, :] for ref in before] + [total[:1]]
        totals = jnp.concatenate(totals, 1)
        lines = SLOTS // GRANULE
        totals = jnp.concatenate(
            [totals[:, i * GRANULE : (i + 1) * GRANULE] for i in range(lines)], 0
        )
        parts = [part.astype(F32) for part in split3(totals)]
        parts.append(jnp.zeros((PART - 3 * lines, GRANULE), F32))
        message_ref[:, size:] = jnp.concatenate(parts, 0).astype(BF16)


def join(keep, came, before, final):
    size = keep.shape[1]
    more = GRANULE if final else 0
    before = before if final else ()
    return pl.pallas_call(
        join_body,
        in_specs=[WHOLE] * (2 + len(before)),
        out_specs=[WHOLE] * 2,
        out_shape=(
            jax.ShapeDtypeStruct((PART + 8, size), F32),
            jax.ShapeDtypeStruct((PART, size + more), BF16),
        ),
        compiler_params=SMALL,
        cost_estimate=pl.CostEstimate(flops=10**6, bytes_accessed=3 * 10**6, transcendentals=0),
        name="join",
    )(keep, came, *before)


def finish_body(live_ref, *refs):
    halves, (log_ref, mean_ref) = refs[:-2], refs[-2:]
    lines = SLOTS // GRANULE
    extra = halves[-1][:, PIECES[-1] :].astype(F32)
    others = extra[:lines] + extra[lines : 2 * lines] + extra[2 * lines : 3 * lines]
    begin = 0
    for part, size in enumerate(PIECES):
        sum_ref, came_ref = halves[2 * part : 2 * part + 2]
        columns = slice(begin, begin + size)
        line = range(begin // GRANULE, (begin + size) // GRANULE)
        begin += size
        total = jnp.concatenate([others[i : i + 1] for i in line], 1)
        total = sum_ref[PART : PART + 1, :] + total
        live = live_ref[:, columns].astype(F32)
        shifted = total + EPSILON
        log_ref[:, columns] = live * jnp.log(shifted)
        scale = live / shifted
        mean_ref[:, columns] = (sum_ref[:PART, :] + came_ref[:, :size].astype(F32)) * scale


def finish(live, halves):
    vmem = pl.BlockSpec(memory_space=pltpu.VMEM)
    return pl.pallas_call(
        finish_body,
        in_specs=[vmem] * (1 + 2 * len(PIECES)),
        out_specs=(vmem, vmem),
        out_shape=(
            jax.ShapeDtypeStruct((1, SLOTS), F32),
            jax.ShapeDtypeStruct((PART, SLOTS), F32),
        ),
        compiler_params=SMALL,
        name="finish",
    )(live.reshape(1, SLOTS), *halves)


def route(blocks, reps, move):
    pairs = []
    for block in range(blocks):
        for rep in range(reps):
            row, column = divmod(block, 2)
            (row_to, column_to), rep_to = move(row, column, rep)
            block_to = (row_to * 2 + column_to) % blocks
            pairs.append((block * reps + rep, block_to * reps + rep_to))
    return pairs


def on_device(embeddings, counts, validity):
    blocks, reps = lax.axis_size("blk"), lax.axis_size("rep")

    def send(value, move):
        return lax.ppermute(value, ("blk", "rep"), route(blocks, reps, move))

    ahead = lambda m, h, r: ((m + 2 * h - 1, h), r)
    behind = lambda m, h, r: ((m + 1 - 2 * h, h), r)
    across = lambda m, h, r: ((m, 1 - h), r ^ 2)
    corner = lambda m, h, r: ((m + 2 * h - 1, 1 - h), r ^ 2)
    other_core = lambda m, h, r: ((m, h), r ^ 1)
    other_chip = lambda m, h, r: ((m, h), r ^ 2)

    mine, live = pack(counts, embeddings, validity)
    from_across = send(mine, across)
    from_ahead = send(mine, ahead)
    from_behind = send(mine, behind)
    *sums, bias = first(embeddings, mine)
    far = send(from_ahead, corner)
    side = send(from_ahead, across)
    near = send(from_across, ahead)
    sums = middle(embeddings, bias, sums, (from_across, from_ahead, from_behind))
    sums = middle(embeddings, bias, sums, (far,))
    halves, begin = [], 0
    for size in PIECES:
        keep, give = last(embeddings, bias, sums, (side, near), begin, size)
        begin += size
        summed, message = join(keep, send(give, other_core), halves[::2], begin == SLOTS)
        halves += [summed, send(message, other_chip)]
    log_density, mean = finish(live, halves)
    return log_density.reshape(SLOTS), mean.T


def solution(mesh):
    return jax.shard_map(
        on_device,
        mesh=mesh,
        in_specs=(P("blk", None), P("blk"), P("blk")),
        out_specs=(P("blk"), P("blk", "rep")),
        check_vma=False,
    )
```

```python
import functools
import math

import jax
import jax.numpy as jnp
from jax import lax
from jax.experimental import pallas as pl
from jax.experimental.pallas import tpu as pltpu
from jax.sharding import PartitionSpec as P

BETA = 8.0
EPSILON = 1e-06
LOG2E = math.log2(math.e)
DEAD = -1e30

SLOTS = 2048
WIDTH = 256
SHARE = 512
GRANULE = 128
EXTRA = 16
TILE = 512
PART = 64
PIECES = (1280, 768)

F32 = jnp.float32
BF16 = jnp.bfloat16
NT = (((1,), (1,)), ((), ()))
VMEM_LIMIT = 32 * 2**20

CROSS = 2.0 * BETA / WIDTH * LOG2E
ROW = -BETA / WIDTH * LOG2E
TOP = 2.0 * BETA * LOG2E


def split3(value):
    high = value.astype(BF16)
    rest = value - high.astype(F32)
    middle = rest.astype(BF16)
    low = (rest - middle.astype(F32)).astype(BF16)
    return high, middle, low


def own_turn():
    return (lax.axis_index("rep") + lax.axis_index("blk")) % 4


def pack_body(counts_ref, embeddings_ref, validity_ref, message_ref, live_ref, count_ref, sems):
    turn = own_turn()
    copies = [
        pltpu.make_async_copy(
            embeddings_ref.at[pl.ds(pl.multiple_of((4 * k + turn) * GRANULE, GRANULE), GRANULE), :],
            message_ref.at[pl.ds(k * GRANULE, GRANULE), :],
            sems.at[k],
        )
        for k in range(4)
    ]
    copies.append(pltpu.make_async_copy(counts_ref, count_ref, sems.at[4]))
    copies.append(pltpu.make_async_copy(validity_ref, live_ref, sems.at[5]))
    for copy in copies:
        copy.start()
    for copy in copies:
        copy.wait()
    rows = message_ref[:SHARE, :].astype(F32)
    square = rows * rows
    square = square[:, :GRANULE] + square[:, GRANULE:]
    norm = jnp.sum(square.T, axis=0, keepdims=True)
    shape = (SLOTS // GRANULE, GRANULE)
    position = lax.broadcasted_iota(jnp.int32, shape, 0) * GRANULE
    position = position + lax.broadcasted_iota(jnp.int32, shape, 1)
    live_ref[...] = jnp.where((position < count_ref[0]) & (live_ref[...] == 1), 1, 0)
    biases = []
    for k in range(4):
        live = live_ref[pl.ds(4 * k + turn, 1), :] == 1
        biases.append(jnp.where(live, TOP + ROW * norm[:, k * GRANULE : (k + 1) * GRANULE], DEAD))
    pairs = [jnp.concatenate(biases[:2], 1), jnp.concatenate(biases[2:], 1)]
    parts = [split3(pair) for pair in pairs]
    lines = [parts[h][level].astype(F32) for level in range(3) for h in range(2)]
    filled = jnp.clip((count_ref[0] // GRANULE - turn + 3) // 4, 0, 4)
    lines.append(jnp.full((EXTRA - 6, WIDTH), filled.astype(F32)))
    message_ref[SHARE:, :] = jnp.concatenate(lines, 0).astype(BF16)


def pack(counts, embeddings, validity):
    vmem = pl.BlockSpec(memory_space=pltpu.VMEM)
    return pl.pallas_call(
        pack_body,
        in_specs=[pl.BlockSpec(memory_space=pl.ANY)] * 3,
        out_specs=(vmem, vmem),
        out_shape=(
            jax.ShapeDtypeStruct((SHARE + EXTRA, WIDTH), BF16),
            jax.ShapeDtypeStruct((SLOTS // GRANULE, GRANULE), jnp.int32),
        ),
        scratch_shapes=[pltpu.SMEM((1,), jnp.int32), pltpu.SemaphoreType.DMA((6,))],
        compiler_params=pltpu.CompilerParams(vmem_limit_bytes=53 * 2**20),
        name="pack",
    )(counts, embeddings, validity.reshape(SLOTS // GRANULE, GRANULE))


def query_bias(query):
    wide = query.astype(F32)
    return jnp.sum(wide * wide, axis=1, keepdims=True) * ROW


def first_body(query_ref, message_ref, total_ref, weighted_ref, bias_ref):
    query = query_ref[...]
    row_bias = jnp.broadcast_to(query_bias(query), (TILE, GRANULE))
    bias_ref[...] = row_bias
    row_bias = jnp.concatenate([row_bias, row_bias], 1)
    extra = message_ref[SHARE:, :].astype(F32)
    half = SHARE // 2
    shape = (TILE, GRANULE)
    offset = lax.broadcasted_iota(jnp.int32, shape, 0) - lax.broadcasted_iota(jnp.int32, shape, 1)
    shift = own_turn() * GRANULE
    for h in range(2):
        rows = message_ref[h * half : (h + 1) * half, :]
        bias = extra[h : h + 1] + extra[2 + h : 3 + h] + extra[4 + h : 5 + h]
        gram = lax.dot_general(query, rows, NT, preferred_element_type=F32)
        kernel = jnp.exp2(gram * CROSS + (row_bias + bias))
        pieces = []
        for j in range(2):
            here = jnp.where(pl.program_id(0) == 2 * h + j, shift, SLOTS)
            piece = kernel[:, j * GRANULE : (j + 1) * GRANULE]
            pieces.append(jnp.where(offset == here, 0.0, piece))
        kernel = jnp.concatenate(pieces, 1)
        total = pieces[0] + pieces[1]
        weighted = jnp.dot(kernel.astype(BF16), rows, preferred_element_type=F32)
        if h == 0:
            total_ref[...] = total
            weighted_ref[...] = weighted
        else:
            total_ref[...] += total
            weighted_ref[...] += weighted


def cut(begin, size):
    step = TILE if size % TILE == 0 else size // 2
    return [slice(at, at + step) for at in range(begin, begin + size, step)]


def collect(messages, rows_ref, cols_ref):
    rows_ref[...] = jnp.zeros_like(rows_ref)
    cols_ref[...] = jnp.full_like(cols_ref, DEAD)
    place = jnp.int32(0)
    for message_ref in messages:
        extra = message_ref[SHARE:, :].astype(F32)
        filled = jnp.max(extra[6:7]).astype(jnp.int32)
        for k in range(4):
            start = pl.multiple_of((place + k) * GRANULE, GRANULE)
            rows_ref[pl.ds(start, GRANULE), :] = message_ref[k * GRANULE : (k + 1) * GRANULE, :]
            h, lanes = k // 2, slice((k % 2) * GRANULE, (k % 2 + 1) * GRANULE)
            bias = extra[h : h + 1, lanes] + extra[2 + h : 3 + h, lanes] + extra[4 + h : 5 + h, lanes]
            cols_ref[pl.ds(place + k, 1), :] = bias
        place = place + filled
    return (place + 1) // 2


def accumulate(pairs, chunks, base, query_ref, bias_ref, rows_ref, cols_ref, total_ref, weighted_ref):
    def run(begin, count):
        for i in range(count):
            pair = begin + i
            start = pl.multiple_of(pair * 2 * GRANULE, 2 * GRANULE)
            rows = rows_ref[pl.ds(start, 2 * GRANULE), :]
            bias = [cols_ref[pl.ds(2 * pair + j, 1), :] for j in range(2)]
            bias = jnp.concatenate(bias, 1)
            for here in chunks:
                there = slice(here.start - base, here.stop - base)
                row_bias = bias_ref[here, :]
                row_bias = jnp.concatenate([row_bias, row_bias], 1)
                gram = lax.dot_general(query_ref[here, :], rows, NT, preferred_element_type=F32)
                kernel = jnp.exp2(gram * CROSS + (row_bias + bias))
                total_ref[there, :] += kernel[:, :GRANULE] + kernel[:, GRANULE:]
                weighted_ref[there, :] += jnp.dot(
                    kernel.astype(BF16), rows, preferred_element_type=F32
                )

    done = jnp.int32(0)
    room = rows_ref.shape[0] // (2 * GRANULE)
    for count in [count for count in (4, 2, 1) if count <= room]:
        fits = pairs - done >= count
        pl.when(fits)(functools.partial(run, done, count))
        done = done + jnp.where(fits, count, 0)


def middle_body(shares, query_ref, bias_ref, total_in, weighted_in, *refs):
    messages, (total_ref, weighted_ref, rows_ref, cols_ref) = refs[:shares], refs[shares:]
    pairs = collect(messages, rows_ref, cols_ref)
    chunks = cut(0, SLOTS)
    accumulate(pairs, chunks, 0, query_ref, bias_ref, rows_ref, cols_ref, total_ref, weighted_ref)


def last_body(shares, begin, size, query_ref, bias_ref, total_in, weighted_in, *refs):
    messages = refs[:shares]
    keep_ref, send_ref, rows_ref, cols_ref, total_ref, weighted_ref = refs[shares:]
    whole = slice(begin, begin + size)
    total_ref[...] = total_in[whole, :]
    weighted_ref[...] = weighted_in[whole, :]
    pairs = collect(messages, rows_ref, cols_ref)
    chunks = cut(begin, size)
    accumulate(
        pairs, chunks, begin, query_ref, bias_ref, rows_ref, cols_ref, total_ref, weighted_ref
    )
    core = lax.axis_index("rep") % 2
    for here in chunks:
        there = slice(here.start - begin, here.stop - begin)
        total = jnp.sum(total_ref[there, :].T, axis=0, keepdims=True)
        total = jnp.broadcast_to(total, (8, total.shape[1]))
        turned = weighted_ref[there, :].T
        quarter = [turned[PART * i : PART * (i + 1)] for i in range(4)]
        for half in range(2):
            first, second = quarter[2 * half], quarter[2 * half + 1]
            keep_ref[PART * half : PART * (half + 1), there] = jnp.where(core == 0, first, second)
            send_ref[PART * half : PART * (half + 1), there] = jnp.where(core == 0, second, first)
        keep_ref[2 * PART :, there] = total
        send_ref[2 * PART :, there] = total


def cost(shares):
    return pl.CostEstimate(
        flops=int(shares * 4 * SLOTS * SHARE * WIDTH),
        bytes_accessed=4 * SLOTS * (WIDTH + GRANULE) * 2,
        transcendentals=int(shares * SLOTS * SHARE),
    )


WHOLE = pl.BlockSpec(memory_space=pltpu.VMEM)
QUERY = pl.BlockSpec((TILE, WIDTH), lambda i: (i, 0))
TOTAL = pl.BlockSpec((TILE, GRANULE), lambda i: (i, 0))
MESSAGE = pl.BlockSpec((SHARE + EXTRA, WIDTH), lambda i: (0, 0))
SUMS = (
    jax.ShapeDtypeStruct((SLOTS, GRANULE), F32),
    jax.ShapeDtypeStruct((SLOTS, WIDTH), F32),
)
PARAMS = pltpu.CompilerParams(vmem_limit_bytes=VMEM_LIMIT)
SMALL = pltpu.CompilerParams(vmem_limit_bytes=16 * 2**20)


def first(query, message):
    return pl.pallas_call(
        first_body,
        grid=(SLOTS // TILE,),
        in_specs=[QUERY, MESSAGE],
        out_specs=(TOTAL, QUERY, TOTAL),
        out_shape=SUMS + (jax.ShapeDtypeStruct((SLOTS, GRANULE), F32),),
        compiler_params=PARAMS,
        cost_estimate=cost(1),
        name="first",
    )(query, message)


def line_up(shares):
    return [((4 * shares * GRANULE, WIDTH), BF16), ((4 * shares, GRANULE), F32)]


def middle(query, bias, sums, messages):
    shares = len(messages)
    return pl.pallas_call(
        functools.partial(middle_body, shares),
        in_specs=[WHOLE] * (4 + shares),
        out_specs=(WHOLE, WHOLE),
        out_shape=SUMS,
        scratch_shapes=[pltpu.VMEM(*spec) for spec in line_up(shares)],
        input_output_aliases={2: 0, 3: 1},
        compiler_params=PARAMS,
        cost_estimate=cost(shares),
        name="middle",
    )(query, bias, *sums, *messages)


def last(query, bias, sums, messages, begin, size):
    shares = len(messages)
    shape = jax.ShapeDtypeStruct((2 * PART + 8, size), F32)
    scratch = line_up(shares) + [((size, GRANULE), F32), ((size, WIDTH), F32)]
    return pl.pallas_call(
        functools.partial(last_body, shares, begin, size),
        in_specs=[WHOLE] * (4 + shares),
        out_specs=(WHOLE, WHOLE),
        out_shape=(shape, shape),
        scratch_shapes=[pltpu.VMEM(*spec) for spec in scratch],
        compiler_params=PARAMS,
        cost_estimate=cost(len(messages) * size / SLOTS),
        name="last",
    )(query, bias, *sums, *messages)


def join_body(keep_ref, came_ref, *refs):
    *before, sum_ref, message_ref = refs
    size = keep_ref.shape[1]
    chip = lax.axis_index("rep") // 2
    both = keep_ref[...] + came_ref[...]
    low, high = both[:PART], both[PART : 2 * PART]
    total = both[2 * PART :]
    sum_ref[:PART, :] = jnp.where(chip == 0, low, high)
    sum_ref[PART:, :] = total
    message_ref[:, :size] = jnp.where(chip == 0, high, low).astype(BF16)
    if message_ref.shape[1] > size:
        totals = [ref[PART : PART + 1, :] for ref in before] + [total[:1]]
        totals = jnp.concatenate(totals, 1)
        lines = SLOTS // GRANULE
        totals = jnp.concatenate(
            [totals[:, i * GRANULE : (i + 1) * GRANULE] for i in range(lines)], 0
        )
        parts = [part.astype(F32) for part in split3(totals)]
        parts.append(jnp.zeros((PART - 3 * lines, GRANULE), F32))
        message_ref[:, size:] = jnp.concatenate(parts, 0).astype(BF16)


def join(keep, came, before, final):
    size = keep.shape[1]
    more = GRANULE if final else 0
    before = before if final else ()
    return pl.pallas_call(
        join_body,
        in_specs=[WHOLE] * (2 + len(before)),
        out_specs=[WHOLE] * 2,
        out_shape=(
            jax.ShapeDtypeStruct((PART + 8, size), F32),
            jax.ShapeDtypeStruct((PART, size + more), BF16),
        ),
        compiler_params=SMALL,
        cost_estimate=pl.CostEstimate(flops=10**6, bytes_accessed=3 * 10**6, transcendentals=0),
        name="join",
    )(keep, came, *before)


def finish_body(live_ref, *refs):
    halves, (log_ref, mean_ref) = refs[:-2], refs[-2:]
    lines = SLOTS // GRANULE
    extra = halves[-1][:, PIECES[-1] :].astype(F32)
    others = extra[:lines] + extra[lines : 2 * lines] + extra[2 * lines : 3 * lines]
    begin = 0
    for part, size in enumerate(PIECES):
        sum_ref, came_ref = halves[2 * part : 2 * part + 2]
        columns = slice(begin, begin + size)
        line = range(begin // GRANULE, (begin + size) // GRANULE)
        begin += size
        total = jnp.concatenate([others[i : i + 1] for i in line], 1)
        total = sum_ref[PART : PART + 1, :] + total
        live = live_ref[:, columns].astype(F32)
        shifted = total + EPSILON
        log_ref[:, columns] = live * jnp.log(shifted)
        scale = live / shifted
        mean_ref[:, columns] = (sum_ref[:PART, :] + came_ref[:, :size].astype(F32)) * scale


def finish(live, halves):
    vmem = pl.BlockSpec(memory_space=pltpu.VMEM)
    return pl.pallas_call(
        finish_body,
        in_specs=[vmem] * (1 + 2 * len(PIECES)),
        out_specs=(vmem, vmem),
        out_shape=(
            jax.ShapeDtypeStruct((1, SLOTS), F32),
            jax.ShapeDtypeStruct((PART, SLOTS), F32),
        ),
        compiler_params=SMALL,
        name="finish",
    )(live.reshape(1, SLOTS), *halves)


def route(blocks, reps, move):
    pairs = []
    for block in range(blocks):
        for rep in range(reps):
            row, column = divmod(block, 2)
            (row_to, column_to), rep_to = move(row, column, rep)
            block_to = (row_to * 2 + column_to) % blocks
            pairs.append((block * reps + rep, block_to * reps + rep_to))
    return pairs


def on_device(embeddings, counts, validity):
    blocks, reps = lax.axis_size("blk"), lax.axis_size("rep")

    def send(value, move):
        return lax.ppermute(value, ("blk", "rep"), route(blocks, reps, move))

    ahead = lambda m, h, r: ((m + 2 * h - 1, h), r)
    behind = lambda m, h, r: ((m + 1 - 2 * h, h), r)
    across = lambda m, h, r: ((m, 1 - h), r ^ 2)
    corner = lambda m, h, r: ((m + 2 * h - 1, 1 - h), r ^ 2)
    other_core = lambda m, h, r: ((m, h), r ^ 1)
    other_chip = lambda m, h, r: ((m, h), r ^ 2)

    mine, live = pack(counts, embeddings, validity)
    from_across = send(mine, across)
    from_ahead = send(mine, ahead)
    from_behind = send(mine, behind)
    *sums, bias = first(embeddings, mine)
    far = send(from_ahead, corner)
    side = send(from_ahead, across)
    near = send(from_across, ahead)
    sums = middle(embeddings, bias, sums, (from_across, from_ahead, from_behind))
    sums = middle(embeddings, bias, sums, (far,))
    halves, begin = [], 0
    for size in PIECES:
        keep, give = last(embeddings, bias, sums, (side, near), begin, size)
        begin += size
        summed, message = join(keep, send(give, other_core), halves[::2], begin == SLOTS)
        halves += [summed, send(message, other_chip)]
    log_density, mean = finish(live, halves)
    return log_density.reshape(SLOTS), mean.T


def solution(mesh):
    return jax.shard_map(
        on_device,
        mesh=mesh,
        in_specs=(P("blk", None), P("blk"), P("blk")),
        out_specs=(P("blk"), P("blk", "rep")),
        check_vma=False,
    )
```

```python
import functools
import math

import jax
import jax.numpy as jnp
from jax import lax
from jax.experimental import pallas as pl
from jax.experimental.pallas import tpu as pltpu
from jax.sharding import PartitionSpec as P

BETA = 8.0
EPSILON = 1e-06
LOG2E = math.log2(math.e)
DEAD = -1e30

SLOTS = 2048
WIDTH = 256
SHARE = 512
GRANULE = 128
EXTRA = 16
TILE = 512
PART = 64
PIECES = (1280, 768)

F32 = jnp.float32
BF16 = jnp.bfloat16
NT = (((1,), (1,)), ((), ()))
VMEM_LIMIT = 32 * 2**20

CROSS = 2.0 * BETA / WIDTH * LOG2E
ROW = -BETA / WIDTH * LOG2E
TOP = 2.0 * BETA * LOG2E


def split3(value):
    high = value.astype(BF16)
    rest = value - high.astype(F32)
    middle = rest.astype(BF16)
    low = (rest - middle.astype(F32)).astype(BF16)
    return high, middle, low


def as_rows(line):
    parts = [part.astype(F32) for part in split3(line)]
    parts.append(jnp.zeros((EXTRA - 3, line.shape[1]), F32))
    return jnp.concatenate(parts, 0).astype(BF16)


def own_turn():
    return (lax.axis_index("rep") + lax.axis_index("blk")) % 4


def pack_body(counts_ref, embeddings_ref, validity_ref, message_ref, live_ref, count_ref, sems):
    turn = own_turn()
    copies = [
        pltpu.make_async_copy(
            embeddings_ref.at[pl.ds(pl.multiple_of((4 * k + turn) * GRANULE, GRANULE), GRANULE), :],
            message_ref.at[pl.ds(k * GRANULE, GRANULE), :],
            sems.at[k],
        )
        for k in range(4)
    ]
    copies.append(pltpu.make_async_copy(counts_ref, count_ref, sems.at[4]))
    copies.append(pltpu.make_async_copy(validity_ref, live_ref, sems.at[5]))
    for copy in copies:
        copy.start()
    for copy in copies:
        copy.wait()
    rows = message_ref[:SHARE, :].astype(F32)
    square = rows * rows
    square = square[:, :GRANULE] + square[:, GRANULE:]
    norm = jnp.sum(square.T, axis=0, keepdims=True)
    shape = (SLOTS // GRANULE, GRANULE)
    position = lax.broadcasted_iota(jnp.int32, shape, 0) * GRANULE
    position = position + lax.broadcasted_iota(jnp.int32, shape, 1)
    live_ref[...] = jnp.where((position < count_ref[0]) & (live_ref[...] == 1), 1, 0)
    biases = []
    for k in range(4):
        live = live_ref[pl.ds(4 * k + turn, 1), :] == 1
        biases.append(jnp.where(live, TOP + ROW * norm[:, k * GRANULE : (k + 1) * GRANULE], DEAD))
    pairs = [jnp.concatenate(biases[:2], 1), jnp.concatenate(biases[2:], 1)]
    parts = [split3(pair) for pair in pairs]
    lines = [parts[h][level].astype(F32) for level in range(3) for h in range(2)]
    filled = jnp.clip((count_ref[0] // GRANULE - turn + 3) // 4, 0, 4)
    lines.append(jnp.full((EXTRA - 6, WIDTH), filled.astype(F32)))
    message_ref[SHARE:, :] = jnp.concatenate(lines, 0).astype(BF16)


def pack(counts, embeddings, validity):
    vmem = pl.BlockSpec(memory_space=pltpu.VMEM)
    return pl.pallas_call(
        pack_body,
        in_specs=[pl.BlockSpec(memory_space=pl.ANY)] * 3,
        out_specs=(vmem, vmem),
        out_shape=(
            jax.ShapeDtypeStruct((SHARE + EXTRA, WIDTH), BF16),
            jax.ShapeDtypeStruct((SLOTS // GRANULE, GRANULE), jnp.int32),
        ),
        scratch_shapes=[pltpu.SMEM((1,), jnp.int32), pltpu.SemaphoreType.DMA((6,))],
        compiler_params=pltpu.CompilerParams(vmem_limit_bytes=53 * 2**20),
        name="pack",
    )(counts, embeddings, validity.reshape(SLOTS // GRANULE, GRANULE))


def query_bias(query):
    wide = query.astype(F32)
    return jnp.sum(wide * wide, axis=1, keepdims=True) * ROW


def first_body(query_ref, message_ref, total_ref, weighted_ref, bias_ref):
    query = query_ref[...]
    row_bias = jnp.broadcast_to(query_bias(query), (TILE, GRANULE))
    bias_ref[...] = row_bias
    row_bias = jnp.concatenate([row_bias, row_bias], 1)
    extra = message_ref[SHARE:, :].astype(F32)
    half = SHARE // 2
    shape = (TILE, GRANULE)
    offset = lax.broadcasted_iota(jnp.int32, shape, 0) - lax.broadcasted_iota(jnp.int32, shape, 1)
    shift = own_turn() * GRANULE
    for h in range(2):
        rows = message_ref[h * half : (h + 1) * half, :]
        bias = extra[h : h + 1] + extra[2 + h : 3 + h] + extra[4 + h : 5 + h]
        gram = lax.dot_general(query, rows, NT, preferred_element_type=F32)
        kernel = jnp.exp2(gram * CROSS + (row_bias + bias))
        pieces = []
        for j in range(2):
            here = jnp.where(pl.program_id(0) == 2 * h + j, shift, SLOTS)
            piece = kernel[:, j * GRANULE : (j + 1) * GRANULE]
            pieces.append(jnp.where(offset == here, 0.0, piece))
        kernel = jnp.concatenate(pieces, 1)
        total = pieces[0] + pieces[1]
        weighted = jnp.dot(kernel.astype(BF16), rows, preferred_element_type=F32)
        if h == 0:
            total_ref[...] = total
            weighted_ref[...] = weighted
        else:
            total_ref[...] += total
            weighted_ref[...] += weighted


def cut(begin, size):
    step = TILE if size % TILE == 0 else size // 2
    return [slice(at, at + step) for at in range(begin, begin + size, step)]


def collect(messages, rows_ref, cols_ref):
    rows_ref[...] = jnp.zeros_like(rows_ref)
    cols_ref[...] = jnp.full_like(cols_ref, DEAD)
    place = jnp.int32(0)
    for message_ref in messages:
        extra = message_ref[SHARE:, :].astype(F32)
        filled = jnp.max(extra[6:7]).astype(jnp.int32)
        for k in range(4):
            start = pl.multiple_of((place + k) * GRANULE, GRANULE)
            rows_ref[pl.ds(start, GRANULE), :] = message_ref[k * GRANULE : (k + 1) * GRANULE, :]
            h, lanes = k // 2, slice((k % 2) * GRANULE, (k % 2 + 1) * GRANULE)
            bias = extra[h : h + 1, lanes] + extra[2 + h : 3 + h, lanes] + extra[4 + h : 5 + h, lanes]
            cols_ref[pl.ds(place + k, 1), :] = bias
        place = place + filled
    return (place + 1) // 2


def accumulate(pairs, chunks, base, query_ref, bias_ref, rows_ref, cols_ref, total_ref, weighted_ref):
    def run(begin, count):
        for i in range(count):
            pair = begin + i
            start = pl.multiple_of(pair * 2 * GRANULE, 2 * GRANULE)
            rows = rows_ref[pl.ds(start, 2 * GRANULE), :]
            bias = [cols_ref[pl.ds(2 * pair + j, 1), :] for j in range(2)]
            bias = jnp.concatenate(bias, 1)
            for here in chunks:
                there = slice(here.start - base, here.stop - base)
                row_bias = bias_ref[here, :]
                row_bias = jnp.concatenate([row_bias, row_bias], 1)
                gram = lax.dot_general(query_ref[here, :], rows, NT, preferred_element_type=F32)
                kernel = jnp.exp2(gram * CROSS + (row_bias + bias))
                total_ref[there, :] += kernel[:, :GRANULE] + kernel[:, GRANULE:]
                weighted_ref[there, :] += jnp.dot(
                    kernel.astype(BF16), rows, preferred_element_type=F32
                )

    done = jnp.int32(0)
    room = rows_ref.shape[0] // (2 * GRANULE)
    for count in [count for count in (4, 2, 1) if count <= room]:
        fits = pairs - done >= count
        pl.when(fits)(functools.partial(run, done, count))
        done = done + jnp.where(fits, count, 0)


def middle_body(shares, query_ref, bias_ref, total_in, weighted_in, *refs):
    messages, (total_ref, weighted_ref, rows_ref, cols_ref) = refs[:shares], refs[shares:]
    pairs = collect(messages, rows_ref, cols_ref)
    chunks = cut(0, SLOTS)
    accumulate(pairs, chunks, 0, query_ref, bias_ref, rows_ref, cols_ref, total_ref, weighted_ref)


def last_body(shares, begin, size, query_ref, bias_ref, total_in, weighted_in, *refs):
    messages = refs[:shares]
    keep_ref, send_ref, rows_ref, cols_ref, total_ref, weighted_ref = refs[shares:]
    whole = slice(begin, begin + size)
    total_ref[...] = total_in[whole, :]
    weighted_ref[...] = weighted_in[whole, :]
    pairs = collect(messages, rows_ref, cols_ref)
    chunks = cut(begin, size)
    accumulate(
        pairs, chunks, begin, query_ref, bias_ref, rows_ref, cols_ref, total_ref, weighted_ref
    )
    core = lax.axis_index("rep") % 2
    for here in chunks:
        there = slice(here.start - begin, here.stop - begin)
        total = jnp.sum(total_ref[there, :].T, axis=0, keepdims=True)
        total = jnp.broadcast_to(total, (8, total.shape[1]))
        turned = weighted_ref[there, :].T
        quarter = [turned[PART * i : PART * (i + 1)] for i in range(4)]
        for half in range(2):
            first, second = quarter[2 * half], quarter[2 * half + 1]
            keep_ref[PART * half : PART * (half + 1), there] = jnp.where(core == 0, first, second)
            given = jnp.where(core == 0, second, first).astype(BF16)
            send_ref[PART * half : PART * (half + 1), there] = given
        keep_ref[2 * PART :, there] = total
        send_ref[2 * PART :, there] = as_rows(total[:1])


def cost(shares):
    return pl.CostEstimate(
        flops=int(shares * 4 * SLOTS * SHARE * WIDTH),
        bytes_accessed=4 * SLOTS * (WIDTH + GRANULE) * 2,
        transcendentals=int(shares * SLOTS * SHARE),
    )


WHOLE = pl.BlockSpec(memory_space=pltpu.VMEM)
QUERY = pl.BlockSpec((TILE, WIDTH), lambda i: (i, 0))
TOTAL = pl.BlockSpec((TILE, GRANULE), lambda i: (i, 0))
MESSAGE = pl.BlockSpec((SHARE + EXTRA, WIDTH), lambda i: (0, 0))
SUMS = (
    jax.ShapeDtypeStruct((SLOTS, GRANULE), F32),
    jax.ShapeDtypeStruct((SLOTS, WIDTH), F32),
)
PARAMS = pltpu.CompilerParams(vmem_limit_bytes=VMEM_LIMIT)
SMALL = pltpu.CompilerParams(vmem_limit_bytes=16 * 2**20)


def first(query, message):
    return pl.pallas_call(
        first_body,
        grid=(SLOTS // TILE,),
        in_specs=[QUERY, MESSAGE],
        out_specs=(TOTAL, QUERY, TOTAL),
        out_shape=SUMS + (jax.ShapeDtypeStruct((SLOTS, GRANULE), F32),),
        compiler_params=PARAMS,
        cost_estimate=cost(1),
        name="first",
    )(query, message)


def line_up(shares):
    return [((4 * shares * GRANULE, WIDTH), BF16), ((4 * shares, GRANULE), F32)]


def middle(query, bias, sums, messages):
    shares = len(messages)
    return pl.pallas_call(
        functools.partial(middle_body, shares),
        in_specs=[WHOLE] * (4 + shares),
        out_specs=(WHOLE, WHOLE),
        out_shape=SUMS,
        scratch_shapes=[pltpu.VMEM(*spec) for spec in line_up(shares)],
        input_output_aliases={2: 0, 3: 1},
        compiler_params=PARAMS,
        cost_estimate=cost(shares),
        name="middle",
    )(query, bias, *sums, *messages)


def last(query, bias, sums, messages, begin, size):
    shares = len(messages)
    kept = jax.ShapeDtypeStruct((2 * PART + 8, size), F32)
    given = jax.ShapeDtypeStruct((2 * PART + EXTRA, size), BF16)
    scratch = line_up(shares) + [((size, GRANULE), F32), ((size, WIDTH), F32)]
    return pl.pallas_call(
        functools.partial(last_body, shares, begin, size),
        in_specs=[WHOLE] * (4 + shares),
        out_specs=(WHOLE, WHOLE),
        out_shape=(kept, given),
        scratch_shapes=[pltpu.VMEM(*spec) for spec in scratch],
        compiler_params=PARAMS,
        cost_estimate=cost(len(messages) * size / SLOTS),
        name="last",
    )(query, bias, *sums, *messages)


def join_body(keep_ref, came_ref, *refs):
    *before, sum_ref, message_ref = refs
    size = keep_ref.shape[1]
    chip = lax.axis_index("rep") // 2
    both = keep_ref[: 2 * PART, :] + came_ref[: 2 * PART, :].astype(F32)
    low, high = both[:PART], both[PART:]
    extra = came_ref[2 * PART :, :].astype(F32)
    total = keep_ref[2 * PART :, :] + (extra[0:1] + extra[1:2] + extra[2:3])
    sum_ref[:PART, :] = jnp.where(chip == 0, low, high)
    sum_ref[PART:, :] = total
    message_ref[:, :size] = jnp.where(chip == 0, high, low).astype(BF16)
    if message_ref.shape[1] > size:
        totals = [ref[PART : PART + 1, :] for ref in before] + [total[:1]]
        totals = jnp.concatenate(totals, 1)
        lines = SLOTS // GRANULE
        totals = jnp.concatenate(
            [totals[:, i * GRANULE : (i + 1) * GRANULE] for i in range(lines)], 0
        )
        parts = [part.astype(F32) for part in split3(totals)]
        parts.append(jnp.zeros((PART - 3 * lines, GRANULE), F32))
        message_ref[:, size:] = jnp.concatenate(parts, 0).astype(BF16)


def join(keep, came, before, final):
    size = keep.shape[1]
    more = GRANULE if final else 0
    before = before if final else ()
    return pl.pallas_call(
        join_body,
        in_specs=[WHOLE] * (2 + len(before)),
        out_specs=[WHOLE] * 2,
        out_shape=(
            jax.ShapeDtypeStruct((PART + 8, size), F32),
            jax.ShapeDtypeStruct((PART, size + more), BF16),
        ),
        compiler_params=SMALL,
        cost_estimate=pl.CostEstimate(flops=10**6, bytes_accessed=3 * 10**6, transcendentals=0),
        name="join",
    )(keep, came, *before)


def finish_body(live_ref, *refs):
    halves, (log_ref, mean_ref) = refs[:-2], refs[-2:]
    lines = SLOTS // GRANULE
    extra = halves[-1][:, PIECES[-1] :].astype(F32)
    others = extra[:lines] + extra[lines : 2 * lines] + extra[2 * lines : 3 * lines]
    begin = 0
    for part, size in enumerate(PIECES):
        sum_ref, came_ref = halves[2 * part : 2 * part + 2]
        columns = slice(begin, begin + size)
        line = range(begin // GRANULE, (begin + size) // GRANULE)
        begin += size
        total = jnp.concatenate([others[i : i + 1] for i in line], 1)
        total = sum_ref[PART : PART + 1, :] + total
        live = live_ref[:, columns].astype(F32)
        shifted = total + EPSILON
        log_ref[:, columns] = live * jnp.log(shifted)
        scale = live / shifted
        mean_ref[:, columns] = (sum_ref[:PART, :] + came_ref[:, :size].astype(F32)) * scale


def finish(live, halves):
    vmem = pl.BlockSpec(memory_space=pltpu.VMEM)
    return pl.pallas_call(
        finish_body,
        in_specs=[vmem] * (1 + 2 * len(PIECES)),
        out_specs=(vmem, vmem),
        out_shape=(
            jax.ShapeDtypeStruct((1, SLOTS), F32),
            jax.ShapeDtypeStruct((PART, SLOTS), F32),
        ),
        compiler_params=SMALL,
        name="finish",
    )(live.reshape(1, SLOTS), *halves)


def route(blocks, reps, move):
    pairs = []
    for block in range(blocks):
        for rep in range(reps):
            row, column = divmod(block, 2)
            (row_to, column_to), rep_to = move(row, column, rep)
            block_to = (row_to * 2 + column_to) % blocks
            pairs.append((block * reps + rep, block_to * reps + rep_to))
    return pairs


def on_device(embeddings, counts, validity):
    blocks, reps = lax.axis_size("blk"), lax.axis_size("rep")

    def send(value, move):
        return lax.ppermute(value, ("blk", "rep"), route(blocks, reps, move))

    ahead = lambda m, h, r: ((m + 2 * h - 1, h), r)
    behind = lambda m, h, r: ((m + 1 - 2 * h, h), r)
    across = lambda m, h, r: ((m, 1 - h), r ^ 2)
    corner = lambda m, h, r: ((m + 2 * h - 1, 1 - h), r ^ 2)
    other_core = lambda m, h, r: ((m, h), r ^ 1)
    other_chip = lambda m, h, r: ((m, h), r ^ 2)

    mine, live = pack(counts, embeddings, validity)
    from_across = send(mine, across)
    from_ahead = send(mine, ahead)
    from_behind = send(mine, behind)
    *sums, bias = first(embeddings, mine)
    far = send(from_ahead, corner)
    side = send(from_ahead, across)
    near = send(from_across, ahead)
    sums = middle(embeddings, bias, sums, (from_across, from_ahead, from_behind))
    sums = middle(embeddings, bias, sums, (far,))
    halves, begin = [], 0
    for size in PIECES:
        keep, give = last(embeddings, bias, sums, (side, near), begin, size)
        begin += size
        summed, message = join(keep, send(give, other_core), halves[::2], begin == SLOTS)
        halves += [summed, send(message, other_chip)]
    log_density, mean = finish(live, halves)
    return log_density.reshape(SLOTS), mean.T


def solution(mesh):
    return jax.shard_map(
        on_device,
        mesh=mesh,
        in_specs=(P("blk", None), P("blk"), P("blk")),
        out_specs=(P("blk"), P("blk", "rep")),
        check_vma=False,
    )
```
